512 devices in a mesh: tok: 32 (over y, z_hi, x), tp: 16 (over z_lo, core).
Axes of the slice: x: 4, y: 4, z: 16 (z_hi: 2, z_lo: 8; z = z_hi * 8 + z_lo), core: 2. Of those that a mesh axis runs over, the one named last changes fastest.
Arguments:
- keys: bfloat16 [4, 1024, 8192], P(None, 'tok', 'tp'), may hold values from -6 to 6
- values: bfloat16 [4, 1024, 3072], P(None, 'tok', 'tp'), may hold values from -6 to 6
- cotangent: bfloat16 [4, 1024, 3072], P(None, 'tok'), may hold values from -0.09375 to 0.09375
- init_weight: bfloat16 [8192, 3072], P('tp'), may hold values from -0.0625 to 0.0625
Outputs:
- layer_out: bfloat16 [4, 1024, 3072], P(None, 'tok', 'tp')
- grad_init: bfloat16 [8192, 3072], P('tp', 'tok')
The draws below stay inside these ranges and needn't reach their ends.
All inputs are finite; a program needn't handle non-finite values.
Results may differ from the reference program's by a relative error of at most 0.02.
Values may be sent and summed in bfloat16 or wider, within the bound.
A program may use at most 64 MiB of HBM per device.

```python
import math
import jax
import jax.numpy as jnp
from jax import lax

D = 3072
FF = 8192
STEPS = 4
BATCH = 1024
N_TOK = 32


def draw_keys(key, part):
    key = jax.random.fold_in(key, 11)
    noise_key = jax.random.fold_in(key, 0)
    field = jnp.clip(jax.random.normal(noise_key, (STEPS, BATCH, FF), jnp.float32), -6.0, 6.0)
    return field.astype(jnp.bfloat16)


def steps_of(rng, dims, shards, least, top_value):
    gain = 1.0
    for position, blocks in shards:
        draws = jax.random.uniform(jax.random.fold_in(jax.random.fold_in(rng, 6), position), (blocks,), jnp.float32, least / len(shards), top_value / len(shards))
        gain = gain * jnp.repeat(jnp.exp(draws), dims[position] // blocks).reshape((-1,) + (1,) * (len(dims) - 1 - position))
    return gain


def scatter_about(stream_key, shape, deviation, limit, cuts=(), held_as=jnp.bfloat16):
    entries = deviation * jax.random.normal(stream_key, shape, jnp.float32)
    if cuts:
        entries = entries * steps_of(stream_key, shape, cuts, -0.22, 0.18)
    return jnp.clip(entries, -limit, limit).astype(held_as)


def setup_inputs(seed: int = 0) -> dict:
    key_of = jax.random.split(jax.random.key(seed), 5)
    keys = draw_keys(jax.random.fold_in(key_of[4], 71), 0)
    values = scatter_about(key_of[1], (STEPS, BATCH, D), 1.0, 6.0, ((1, 32), (2, 16)))
    cotangent = scatter_about(key_of[2], (STEPS, BATCH, D), (STEPS * BATCH) ** -0.5, 0.09375, ((1, 32),))
    init_weight = scatter_about(key_of[3], (FF, D), FF ** -0.5, 0.0625, ((0, 16),))
    return dict(keys=keys, values=values, cotangent=cotangent, init_weight=init_weight)


MOMENTUM = 0.9

def momentum_sum(count):
    return (1.0 - MOMENTUM ** count) / (1.0 - MOMENTUM)

def reference(keys, values, cotangent, init_weight):
    step_count, batch_size, hidden = keys.shape
    model_width = init_weight.shape[1]
    inner_rate = 0.5 * batch_size / (math.sqrt(hidden) + math.sqrt(batch_size)) ** 2
    step_scale = inner_rate / batch_size
    key_rows = keys.reshape(step_count * batch_size, hidden)
    projected = jnp.dot(key_rows, init_weight, preferred_element_type=jnp.float32)
    projected = projected.reshape(step_count, batch_size, model_width)
    all_scores = jnp.dot(key_rows, key_rows.T, preferred_element_type=jnp.float32)
    all_scores = all_scores.reshape(step_count, batch_size, step_count, batch_size)
    residuals = []
    outputs = []
    for t in range(step_count):
        correction = jnp.zeros((batch_size, model_width), jnp.float32)
        for s in range(t):
            weight_block = (step_scale * momentum_sum(t - s) * all_scores[t, :, s, :]).astype(jnp.bfloat16)
            correction = correction + jnp.dot(weight_block, residuals[s], preferred_element_type=jnp.float32)
        residuals.append((projected[t] - correction - values[t].astype(jnp.float32)).astype(jnp.bfloat16))
        mixing = jnp.zeros((batch_size, model_width), jnp.float32)
        for s in range(t + 1):
            weight_block = (step_scale * momentum_sum(t + 1 - s) * all_scores[t, :, s, :]).astype(jnp.bfloat16)
            mixing = mixing + jnp.dot(weight_block, residuals[s], preferred_element_type=jnp.float32)
        outputs.append((projected[t] - mixing).astype(jnp.bfloat16))
    adjoints = [None] * step_count
    for s in reversed(range(step_count)):
        accumulated = jnp.zeros((batch_size, model_width), jnp.float32)
        for t in range(s, step_count):
            weight_block = (step_scale * momentum_sum(t + 1 - s) * all_scores[s, :, t, :]).astype(jnp.bfloat16)
            accumulated = accumulated + jnp.dot(weight_block, cotangent[t], preferred_element_type=jnp.float32)
        for t in range(s + 1, step_count):
            weight_block = (step_scale * momentum_sum(t - s) * all_scores[s, :, t, :]).astype(jnp.bfloat16)
            accumulated = accumulated + jnp.dot(weight_block, adjoints[t], preferred_element_type=jnp.float32)
        adjoints[s] = (-accumulated).astype(jnp.bfloat16)
    combined = jnp.stack(adjoints).astype(jnp.float32) + cotangent.astype(jnp.float32)
    mb_rows = batch_size // N_TOK

    def add_group(carry, source):
        start = (source * mb_rows).astype(jnp.int32)
        key_block = lax.dynamic_slice_in_dim(keys, start, mb_rows, 1)
        key_block = key_block.reshape(step_count * mb_rows, hidden).astype(jnp.float32)
        adjoint_block = lax.dynamic_slice_in_dim(combined, start, mb_rows, 1)
        adjoint_block = adjoint_block.reshape(step_count * mb_rows, model_width)
        term = jnp.dot(key_block.T, adjoint_block, precision=lax.Precision.HIGHEST, preferred_element_type=jnp.float32)
        return (carry + lax.optimization_barrier(term.astype(jnp.bfloat16)).astype(jnp.float32), None)
    grad_sum, _ = lax.scan(add_group, jnp.zeros((hidden, model_width), jnp.float32), jnp.arange(N_TOK, dtype=jnp.int32))
    return (jnp.stack(outputs), grad_sum.astype(jnp.bfloat16))
```

```python
import functools
import math

import jax
import jax.numpy as jnp
from jax import lax
from jax.experimental import pallas as pl
from jax.experimental.pallas import tpu as pltpu
from jax.sharding import PartitionSpec as P

MOMENTUM = 0.9
LANES = 128
F32 = jnp.float32
BF16 = jnp.bfloat16
VMEM_LIMIT = 48 * 1024 * 1024


def momentum_sum(count):
    return (1.0 - MOMENTUM**count) / (1.0 - MOMENTUM)


class Grid:
    def __init__(self, side, depth):
        self.side, self.depth, self.area = side, depth, side * side
        tok, tp = lax.axis_index("tok"), lax.axis_index("tp")
        self.tok, self.tp = tok, tp
        self.y = lax.div(tok, 2 * side)
        self.zhi = lax.rem(lax.div(tok, side), 2)
        self.x = lax.rem(tok, side)
        self.zlo = lax.div(tp, 2)
        self.core = lax.rem(tp, 2)
        self.a = self.y * side + self.x
        self.z = self.zhi * depth + self.zlo

    def tok_of(self, y, zhi, x):
        return y * (2 * self.side) + zhi * self.side + x

    def at_xy(self, dy, dx):
        y = lax.rem(self.y + dy + self.side, self.side)
        x = lax.rem(self.x + dx + self.side, self.side)
        return (self.tok_of(y, self.zhi, x), self.tp)

    def a_at(self, dy, dx):
        y = lax.rem(self.y + dy + self.side, self.side)
        x = lax.rem(self.x + dx + self.side, self.side)
        return y * self.side + x

    def partner(self):
        return (self.tok_of(self.y, 1 - self.zhi, self.x), self.tp)

    def sibling(self):
        return (self.tok, self.zlo * 2 + 1 - self.core)

    def zlo_at(self, d):
        return lax.rem(self.zlo + d + self.depth, self.depth)

    def on_line(self, d):
        return (self.tok, self.zlo_at(d) * 2 + self.core)

    def z_at(self, d):
        return lax.rem(self.z + d + 2 * self.depth, 2 * self.depth)

    def on_ring(self, d):
        z = self.z_at(d)
        zhi, zlo = lax.div(z, self.depth), lax.rem(z, self.depth)
        return (self.tok_of(self.y, zhi, self.x), zlo * 2 + self.core)

    def xy_offsets(self):
        return [(dy, dx) for dy in range(self.side) for dx in range(self.side) if (dy, dx) != (0, 0)]

    def line_order(self):
        half = self.depth // 2
        return sorted(range(1, self.depth), key=lambda d: abs(d - half)) + [0]


def remote(src, dst, send, recv, device):
    return pltpu.make_async_remote_copy(
        src_ref=src, dst_ref=dst, send_sem=send, recv_sem=recv, device_id=device, device_id_type=pl.DeviceIdType.MESH
    )


def greet(targets, count):
    barrier = pltpu.get_barrier_semaphore()
    for device in targets:
        pl.semaphore_signal(barrier, inc=1, device_id=device, device_id_type=pl.DeviceIdType.MESH)
    pl.semaphore_wait(barrier, count)


class Wave:
    def __init__(self, grid, blocks, sems):
        side, steps = grid.side, blocks.shape[0]
        half = steps // 2
        self.first, self.second = {}, {}
        send1, recv1, send2, recv2 = sems
        for h in range(2):
            part = pl.ds(h * half, half)
            for d in range(1, side):
                mine = blocks.at[part, grid.a]
                peer = grid.at_xy(d, 0) if h == 0 else grid.at_xy(0, d)
                self.first[h, d] = remote(mine, mine, send1.at[h, d], recv1.at[h, d], peer)
            for d in range(side):
                held = blocks.at[part, grid.a_at(-d, 0) if h == 0 else grid.a_at(0, -d)]
                for e in range(1, side):
                    peer = grid.at_xy(0, e) if h == 0 else grid.at_xy(e, 0)
                    self.second[h, d, e] = remote(held, held, send2.at[h, d, e], recv2.at[h, d, e], peer)
        self.side = side

    def start(self):
        for d in range(1, self.side):
            for h in range(2):
                self.first[h, d].start()
        for e in range(1, self.side):
            for h in range(2):
                self.second[h, 0, e].start()

    def forward(self):
        for d in range(1, self.side):
            for h in range(2):
                self.first[h, d].wait_recv()
                for e in range(1, self.side):
                    self.second[h, d, e].start()

    def finish(self):
        for copy in self.second.values():
            copy.wait_recv()
        for copy in list(self.first.values()) + list(self.second.values()):
            copy.wait_send()


def wave_scratch(side):
    return [pltpu.SemaphoreType.DMA((2, side))] * 2 + [pltpu.SemaphoreType.DMA((2, side, side))] * 2


class LineSum:
    def __init__(self, grid, part, sib_in, stage, recv, sems):
        self.grid, self.part, self.sib_in, self.stage, self.recv = grid, part, sib_in, stage, recv
        sib_send, sib_recv, send, rsem = sems
        self.order = grid.line_order()
        self.sib, self.line = {}, {}
        for d in self.order:
            theirs = part.at[grid.zlo_at(d) * 2 + 1 - grid.core]
            self.sib[d] = remote(theirs, sib_in.at[d], sib_send.at[d], sib_recv.at[d], grid.sibling())
            if d:
                self.line[d] = remote(stage.at[d], recv.at[d], send.at[d], rsem.at[d], grid.on_line(d))

    def pair(self, d):
        own = self.part[self.grid.zlo_at(d) * 2 + self.grid.core]
        return own.astype(F32) + self.sib_in[d].astype(F32)

    def send(self):
        for d in self.order:
            self.sib[d].wait_recv()
            if d:
                self.stage[d] = self.pair(d).astype(BF16)
                self.line[d].start()

    def total(self):
        total = self.pair(0)
        for d in self.order[:-1]:
            self.line[d].wait_recv()
            total = total + self.recv[d].astype(F32)
        return total

    def finish(self):
        for copy in list(self.sib.values()) + list(self.line.values()):
            copy.wait_send()


def line_scratch(depth, rows):
    return [
        pltpu.VMEM((depth, rows, LANES), BF16),
        pltpu.VMEM((depth, rows, LANES), BF16),
        pltpu.VMEM((depth, rows, LANES), BF16),
    ] + [pltpu.SemaphoreType.DMA((depth,))] * 4


def line_devices(grid):
    return [grid.sibling()] + [grid.on_line(d) for d in range(1, grid.depth)]


def gather_kernel(
    side, depth, key_ref, part_ref, vc_ref, kmine, kpair, call, pm, vm,
    total_ref, vc_in, sib_in, stage, recv, ls0, ls1, ls2, ls3, w0, w1, w2, w3, swap_sem, c_send, c_recv,
):
    grid = Grid(side, depth)
    zhi = grid.zhi
    xy = grid.xy_offsets()
    targets = [grid.partner()] + [grid.at_xy(*d) for d in xy] + line_devices(grid)
    greet(targets, len(targets))

    lines = LineSum(grid, part_ref, sib_in, stage, recv, (ls0, ls1, ls2, ls3))
    for d in lines.order:
        lines.sib[d].start()
    vc_swap = remote(vc_ref.at[1 - zhi], vc_in, swap_sem.at[0, 0], swap_sem.at[1, 0], grid.partner())
    vc_swap.start()
    key_swap = remote(key_ref, kpair, swap_sem.at[0, 1], swap_sem.at[1, 1], grid.partner())
    key_swap.start()
    kmine[:, grid.a] = key_ref[...]
    wave = Wave(grid, kmine, (w0, w1, w2, w3))
    wave.start()
    lines.send()
    wave.forward()

    vc_swap.wait()
    vm[zhi] = vc_ref[zhi, 0]
    vm[1 - zhi] = vc_in[0]
    call[:, zhi, grid.a] = vc_ref[zhi, 1]
    call[:, 1 - zhi, grid.a] = vc_in[1]
    mine = call.at[:, :, grid.a]
    spread = [remote(mine, mine, c_send.at[dy, dx], c_recv.at[dy, dx], grid.at_xy(dy, dx)) for dy, dx in xy]
    for copy in spread:
        copy.start()

    total_ref[...] = lines.total().reshape(total_ref.shape)
    pm[zhi] = total_ref[zhi]
    p_swap = remote(total_ref.at[1 - zhi], pm.at[zhi], swap_sem.at[0, 2], swap_sem.at[1, 2], grid.partner())
    p_swap.start()

    for copy in spread:
        copy.wait()
    wave.finish()
    lines.finish()
    key_swap.wait()
    p_swap.wait()


def scores_kernel(
    side, depth, kmine, kpair, kother, sall,
    lhs, part, sib_in, stage, recv, ls0, ls1, ls2, ls3, w0, w1, w2, w3, ring_send, ring_recv, sib_send, sib_recv,
):
    grid = Grid(side, depth)
    zhi = grid.zhi
    targets = [grid.at_xy(d, 0) for d in range(1, side)] + [grid.at_xy(0, d) for d in range(1, side)]
    targets += line_devices(grid) + [grid.on_ring(1), grid.on_ring(-1)]
    greet(targets, len(targets))

    kother[:, grid.a] = kpair[...]
    wave = Wave(grid, kother, (w0, w1, w2, w3))
    wave.start()

    quarters = kmine.shape[1] * kmine.shape[2] // LANES
    width = kmine.shape[3]
    lhs[zhi] = kmine[:, grid.a]
    lhs[1 - zhi] = kpair[...]
    rows = lhs[...].reshape(-1, width)
    lines = LineSum(grid, part, sib_in, stage, recv, (ls0, ls1, ls2, ls3))

    def piece(j):
        s, q = lax.div(j, quarters), lax.rem(j, quarters)
        block = kmine[s, pl.ds(q * 4, 4)].reshape(LANES, width)
        part[j] = lax.dot_general(
            rows, block, (((1,), (1,)), ((), ())), preferred_element_type=F32
        ).astype(BF16)

    for d in lines.order:
        piece(grid.zlo_at(d) * 2 + 1 - grid.core)
        lines.sib[d].start()
    for d in lines.order:
        piece(grid.zlo_at(d) * 2 + grid.core)
    lines.send()
    wave.forward()

    def columns(z):
        half, j = lax.div(z, depth), lax.rem(z, depth) * 2 + grid.core
        s, q = lax.div(j, quarters), lax.rem(j, quarters)
        return sall.at[:, pl.ds(pl.multiple_of((s * 2 + half) * quarters * LANES + q * LANES, LANES), LANES)]

    total = lines.total()
    mine = columns(grid.z)
    mine[...] = total.astype(BF16)

    def hop(step, way):
        held = columns(grid.z_at(-way * step))
        slot = 0 if way > 0 else 1
        return remote(held, held, ring_send.at[slot, step], ring_recv.at[slot, step], grid.on_ring(way))

    def share(z, slot):
        held = columns(z)
        return remote(held, held, sib_send.at[slot], sib_recv.at[slot], grid.sibling())

    copies, shared = [], []

    def go(copy, to):
        copy.start()
        to.append(copy)

    up, down = hop(0, 1), hop(0, -1)
    go(up, copies)
    go(down, copies)
    go(share(grid.z, 0), shared)
    for step in range(depth):
        up.wait_recv()
        if step + 1 < depth:
            up = hop(step + 1, 1)
            go(up, copies)
            down.wait_recv()
            if step + 2 < depth:
                down = hop(step + 1, -1)
                go(down, copies)
        go(share(grid.z_at(-step - 1), 1 + step), shared)
        if step + 1 < depth:
            go(share(grid.z_at(step + 1), 1 + depth + step), shared)
    for copy in shared:
        copy.wait()
    for copy in copies:
        copy.wait_send()
    wave.finish()
    lines.finish()


def rounds_kernel(
    side, depth, scale, sall, pm, vm, call, out, comb,
    msg, xg, acc_f, acc_o, acc_b, tsend, osend,
    x_send, x_recv, t_send, t_recv, l_send, l_recv, s_send, s_recv, o_send, o_recv,
):
    grid = Grid(side, depth)
    zhi, area = grid.zhi, grid.area
    steps = pm.shape[1]
    mb = pm.shape[2]
    xy = grid.xy_offsets()
    holder = (2 * grid.tp + zhi, lax.rem(grid.a + area // 2, area))
    source_tp = lax.div(grid.tok, 2)
    source_a = lax.rem(grid.tp + area // 2, area)
    source = (grid.tok_of(lax.div(source_a, side), lax.rem(grid.tok, 2), lax.rem(source_a, side)), source_tp)
    near = [grid.at_xy(*d) for d in xy] + line_devices(grid) + [grid.partner()]
    greet(near + [source], len(near) + 1)

    scores = sall[...]
    batch = 2 * area * mb

    def product(column, right):
        return jnp.dot(
            scores[:, column * batch:(column + 1) * batch], right.reshape(batch, LANES), preferred_element_type=F32
        ).reshape(2, steps, mb, LANES)

    acc_f[...] = jnp.zeros_like(acc_f)
    acc_o[...] = jnp.zeros_like(acc_o)
    acc_b[...] = jnp.zeros_like(acc_b)

    def from_cotangent(t):
        term = product(t, call[t])
        for s in range(t + 1):
            acc_b[:, s] += (scale * momentum_sum(t + 1 - s)) * term[:, s]

    def line_copies(u):
        slot = comb.at[u, :, source_a]
        out_copies = [
            remote(slot, slot, l_send.at[u, d], l_recv.at[u, d], grid.on_line(d)) for d in range(1, depth)
        ]
        shares = []
        for d in range(depth):
            a = lax.rem(grid.zlo_at(-d) * 2 + grid.core + area // 2, area)
            held = comb.at[u, :, a]
            shares.append(remote(held, held, s_send.at[u, d], s_recv.at[u, d], grid.sibling()))
        return out_copies, shares

    to_holder, lines, shares, spread, given = {}, {}, {}, {}, {}
    from_cotangent(steps - 1)
    for r in range(steps):
        t, u = r, steps - 1 - r
        msg[r, 0] = (pm[:, t] - acc_f[:, t] - vm[:, t].astype(F32)).astype(BF16)
        adjoint = (-acc_b[:, u]).astype(BF16)
        msg[r, 1] = adjoint
        spread[r] = [
            remote(msg.at[r], xg.at[r, :, :, grid.a], x_send.at[r, dy, dx], x_recv.at[r, dy, dx], grid.at_xy(dy, dx))
            for dy, dx in xy
        ]
        for copy in spread[r]:
            copy.start()
        tsend[u] = (adjoint.astype(F32) + call[u, :, grid.a].astype(F32)).astype(BF16)
        to_holder[u] = remote(tsend.at[u], comb.at[u, :, grid.a], t_send.at[u], t_recv.at[u], holder)
        to_holder[u].start()
        xg[r, :, :, grid.a] = msg[r]
        if u > 0:
            from_cotangent(u - 1)
        if r > 0:
            to_holder[u + 1].wait_recv()
            lines[u + 1], shares[u + 1] = line_copies(u + 1)
            for copy in lines[u + 1]:
                copy.start()
            shares[u + 1][0].start()
        if r > 1:
            for d in range(1, depth):
                lines[u + 2][d - 1].wait_recv()
                shares[u + 2][d].start()
        for copy in spread[r]:
            copy.wait_recv()
        forward = product(t, xg[r, 0])
        for row in range(t, steps):
            if row > t:
                acc_f[:, row] += (scale * momentum_sum(row - t)) * forward[:, row]
            acc_o[:, row] += (scale * momentum_sum(row + 1 - t)) * forward[:, row]
        if u > 0:
            backward = product(u, xg[r, 1])
            for row in range(u):
                acc_b[:, row] += (scale * momentum_sum(u - row)) * backward[:, row]
        result = (pm[:, t] - acc_o[:, t]).astype(BF16)
        osend[:, t] = result
        out[zhi, t] = osend[zhi, t]
        given[t] = remote(osend.at[1 - zhi, t], out.at[zhi, t], o_send.at[t], o_recv.at[t], grid.partner())
        given[t].start()

    to_holder[0].wait_recv()
    lines[0], shares[0] = line_copies(0)
    for copy in lines[0]:
        copy.start()
    shares[0][0].start()
    for u in (1, 0):
        for d in range(1, depth):
            lines[u][d - 1].wait_recv()
            shares[u][d].start()
    for u in range(steps):
        for copy in shares[u]:
            copy.wait()
        for copy in lines[u] + spread[u]:
            copy.wait_send()
        to_holder[u].wait_send()
        given[u].wait()


def call_kernel(body, name, identity, outs, scratch, *args):
    vmem = pl.BlockSpec(memory_space=pltpu.VMEM)
    return pl.pallas_call(
        body,
        name=name,
        out_shape=[jax.ShapeDtypeStruct(shape, dtype) for shape, dtype in outs],
        in_specs=[vmem] * len(args),
        out_specs=[vmem] * len(outs),
        scratch_shapes=scratch,
        compiler_params=pltpu.CompilerParams(
            collective_id=identity, has_side_effects=True, vmem_limit_bytes=VMEM_LIMIT
        ),
    )(*args)


def per_device(keys, values, cotangent, init_weight):
    steps, mb, width = keys.shape
    model_width = init_weight.shape[1]
    tok_count, tp_count = lax.axis_size("tok"), lax.axis_size("tp")
    side, depth = math.isqrt(tok_count // 2), tp_count // 2
    area = side * side
    rows = steps * mb
    cols = model_width // (2 * tp_count)
    hidden, batch_size = width * tp_count, mb * tok_count
    inner_rate = 0.5 * batch_size / (math.sqrt(hidden) + math.sqrt(batch_size)) ** 2
    scale = inner_rate / batch_size
    tp = lax.axis_index("tp")
    zhi = lax.rem(lax.div(lax.axis_index("tok"), side), 2)
    dma = pltpu.SemaphoreType.DMA

    def pad(array):
        return jnp.pad(array, [(0, 0)] * (array.ndim - 1) + [(0, LANES - cols)])

    key_rows = keys.reshape(rows, width)
    projected = jnp.dot(key_rows, init_weight, preferred_element_type=F32).astype(BF16)
    projected = pad(projected.reshape(rows, tp_count, 2, cols).transpose(1, 2, 0, 3))
    projected = projected.reshape(tp_count, 2 * rows, LANES)
    cot = lax.dynamic_slice_in_dim(cotangent, tp * 2 * cols, 2 * cols, 2)
    vc = jnp.stack([values, cot]).reshape(2, steps, mb, 2, cols).transpose(3, 0, 1, 2, 4)
    vc = pad(vc)

    kmine, kpair, call, pm, vm = call_kernel(
        functools.partial(gather_kernel, side, depth), "gather", 0,
        [
            ((steps, area, mb, width), BF16), ((steps, mb, width), BF16), ((steps, 2, area, mb, LANES), BF16),
            ((2, steps, mb, LANES), F32), ((2, steps, mb, LANES), BF16),
        ],
        [pltpu.VMEM((2, steps, mb, LANES), F32), pltpu.VMEM((2, steps, mb, LANES), BF16)]
        + line_scratch(depth, 2 * rows) + wave_scratch(side) + [dma((2, 3)), dma((side, side)), dma((side, side))],
        keys, projected, vc,
    )
    kother, sall = call_kernel(
        functools.partial(scores_kernel, side, depth), "scores", 1,
        [((steps, area, mb, width), BF16), ((2 * rows, steps * batch_size), BF16)],
        [pltpu.VMEM((2, steps, mb, width), BF16), pltpu.VMEM((tp_count, 2 * rows, LANES), BF16)]
        + line_scratch(depth, 2 * rows) + wave_scratch(side)
        + [dma((2, depth)), dma((2, depth)), dma((2 * depth,)), dma((2 * depth,))],
        kmine, kpair,
    )
    half = (2, steps, mb, LANES)
    out, comb = call_kernel(
        functools.partial(rounds_kernel, side, depth, scale), "rounds", 2,
        [(half, BF16), ((steps, 2, area, mb, LANES), BF16)],
        [
            pltpu.VMEM((steps, 2, 2, mb, LANES), BF16), pltpu.VMEM((steps, 2, 2, area, mb, LANES), BF16),
            pltpu.VMEM(half, F32), pltpu.VMEM(half, F32), pltpu.VMEM(half, F32),
            pltpu.VMEM((steps, 2, mb, LANES), BF16), pltpu.VMEM(half, BF16),
            dma((steps, side, side)), dma((steps, side, side)), dma((steps,)), dma((steps,)),
            dma((steps, depth)), dma((steps, depth)), dma((steps, depth)), dma((steps, depth)),
            dma((steps,)), dma((steps,)),
        ],
        sall, pm, vm, call,
    )
    layer_out = out[..., :cols].transpose(1, 2, 0, 3).reshape(steps, mb, 2 * cols)

    def gradient(blocks, which):
        right = lax.dynamic_index_in_dim(comb, which, 1, keepdims=False).reshape(-1, LANES)[:, :cols]
        return lax.dot_general(
            blocks.reshape(-1, width), right, (((0,), (0,)), ((), ())), preferred_element_type=F32
        )

    grad = gradient(kmine, zhi) + gradient(kother, 1 - zhi)
    return (layer_out, grad.astype(BF16))


def solution(mesh):
    return jax.shard_map(
        per_device,
        mesh=mesh,
        in_specs=(P(None, "tok", "tp"), P(None, "tok", "tp"), P(None, "tok", None), P("tp", None)),
        out_specs=(P(None, "tok", "tp"), P("tp", "tok")),
        check_vma=False,
    )
```

```python
import functools
import math

import jax
import jax.numpy as jnp
from jax import lax
from jax.experimental import pallas as pl
from jax.experimental.pallas import tpu as pltpu
from jax.sharding import PartitionSpec as P

MOMENTUM = 0.9
LANES = 128
TILE = 16
F32 = jnp.float32
BF16 = jnp.bfloat16
VMEM_LIMIT = 56 * 1024 * 1024
STEPS = 4
SIDE = 4
DEPTH = 8
AREA = SIDE * SIDE
STAGES = (
    ((1, 0), (3, 3)),
    ((2, 0), (2, 1), (2, 2), (2, 3)),
    ((3, 0), (3, 1), (3, 2), (1, 1), (1, 2), (1, 3)),
    ((0, 0), (0, 1), (0, 2), (0, 3)),
)
BLOCKS = [block for stage in STAGES for block in stage]
STARTS = [sum(len(stage) for stage in STAGES[:i]) for i in range(len(STAGES))]


def momentum_sum(count):
    return (1.0 - MOMENTUM**count) / (1.0 - MOMENTUM)


class Grid:
    def __init__(self):
        tok, tp = lax.axis_index("tok"), lax.axis_index("tp")
        self.tok, self.tp = tok, tp
        self.y = lax.div(tok, 2 * SIDE)
        self.zhi = lax.rem(lax.div(tok, SIDE), 2)
        self.x = lax.rem(tok, SIDE)
        self.zlo = lax.div(tp, 2)
        self.core = lax.rem(tp, 2)
        self.a = self.y * SIDE + self.x
        self.z = self.zhi * DEPTH + self.zlo
        self.group = lax.div(self.zlo, 2)
        self.par = lax.rem(self.zlo, 2)
        self.rghi = lax.div(self.zlo, 4)
        self.rglo = lax.rem(self.group, 2)

    def tok_of(self, y, zhi, x):
        return y * (2 * SIDE) + zhi * SIDE + x

    def at_xy(self, dy, dx):
        y = lax.rem(self.y + dy + SIDE, SIDE)
        x = lax.rem(self.x + dx + SIDE, SIDE)
        return (self.tok_of(y, self.zhi, x), self.tp)

    def a_at(self, dy, dx):
        y = lax.rem(self.y + dy + SIDE, SIDE)
        x = lax.rem(self.x + dx + SIDE, SIDE)
        return y * SIDE + x

    def partner(self):
        return (self.tok_of(self.y, 1 - self.zhi, self.x), self.tp)

    def sibling(self):
        return (self.tok, self.zlo * 2 + 1 - self.core)

    def pair(self):
        return (self.tok, (self.zlo + 1 - 2 * self.par) * 2 + self.core)

    def group_at(self, d):
        return lax.rem(self.group + d + DEPTH // 2, DEPTH // 2)

    def on_line(self, d):
        return (self.tok, (self.group_at(d) * 2 + self.par) * 2 + self.core)

    def on_ring(self, d):
        z = lax.rem(self.z + d + 2 * DEPTH, 2 * DEPTH)
        zhi, zlo = lax.div(z, DEPTH), lax.rem(z, DEPTH)
        return (self.tok_of(self.y, zhi, self.x), zlo * 2 + self.core)

    def owners(self):
        core = 1 - lax.div(self.x, 2)
        return [(2 * self.tp + self.zhi, lax.rem(self.zlo + k, DEPTH) * 2 + core) for k in range(DEPTH)]

    def sources(self):
        tp, zhi = lax.div(self.tok, 2), lax.rem(self.tok, 2)
        return [
            (self.tok_of(y, zhi, (1 - self.core) * 2 + x), tp) for y in range(SIDE) for x in range(SIDE // 2)
        ]


XY = [(dy, dx) for dy in range(SIDE) for dx in range(SIDE) if (dy, dx) != (0, 0)]


def remote(src, dst, send, recv, device):
    return pltpu.make_async_remote_copy(
        src_ref=src, dst_ref=dst, send_sem=send, recv_sem=recv, device_id=device, device_id_type=pl.DeviceIdType.MESH
    )


class Wave:
    def __init__(self, grid, blocks, sems, number, first, second):
        self.first, self.second = {}, {}
        send1, recv1, send2, recv2 = [sem.at[number] for sem in sems]
        for h, s in enumerate((first, second)):
            for d in range(1, SIDE):
                mine = blocks.at[s, grid.a]
                peer = grid.at_xy(d, 0) if h == 0 else grid.at_xy(0, d)
                self.first[h, d] = remote(mine, mine, send1.at[h, d], recv1.at[h, d], peer)
            for d in range(SIDE):
                held = blocks.at[s, grid.a_at(-d, 0) if h == 0 else grid.a_at(0, -d)]
                for e in range(1, SIDE):
                    peer = grid.at_xy(0, e) if h == 0 else grid.at_xy(e, 0)
                    self.second[h, d, e] = remote(held, held, send2.at[h, d, e], recv2.at[h, d, e], peer)

    def start(self):
        for d in range(1, SIDE):
            for h in range(2):
                self.first[h, d].start()
        for e in range(1, SIDE):
            for h in range(2):
                self.second[h, 0, e].start()

    def forward(self):
        for d in range(1, SIDE):
            for h in range(2):
                self.first[h, d].wait_recv()
                for e in range(1, SIDE):
                    self.second[h, d, e].start()

    def arrived(self):
        for copy in self.second.values():
            copy.wait_recv()

    def sent(self):
        for copy in list(self.first.values()) + list(self.second.values()):
            copy.wait_send()


class LineSum:
    def __init__(self, grid, bufs, sems, ranges):
        self.grid, self.ranges = grid, ranges
        self.part, self.sib, self.stage1, self.pair, self.stage2, self.recv = bufs
        sib_s, sib_r, pair_s, pair_r, line_s, line_r = sems
        self.sib_copy, self.pair_copy, self.line_copy = [], [], []
        for i, (start, size) in enumerate(ranges):
            b = pl.ds(start, size)
            self.sib_copy.append(remote(
                self.part.at[:, :, 1 - grid.core, b], self.sib.at[:, :, b], sib_s.at[i], sib_r.at[i], grid.sibling()
            ))
            self.pair_copy.append(remote(
                self.stage1.at[:, b], self.pair.at[:, b], pair_s.at[i], pair_r.at[i], grid.pair()
            ))
            self.line_copy.append([
                remote(self.stage2.at[d, b], self.recv.at[d, b], line_s.at[i, d], line_r.at[i, d], grid.on_line(d))
                for d in range(1, DEPTH // 2)
            ])

    def begin(self, i):
        self.sib_copy[i].start()

    def to_pair(self, i):
        grid, b = self.grid, pl.ds(*self.ranges[i])
        self.sib_copy[i].wait_recv()
        other = 1 - grid.par
        own = self.part[:, other, grid.core, b].astype(F32) + self.sib[:, other, b].astype(F32)
        self.stage1[:, b] = own.astype(BF16)
        self.pair_copy[i].start()

    def chip_sum(self, group, b):
        grid = self.grid
        own = self.part[group, grid.par, grid.core, b].astype(F32) + self.sib[group, grid.par, b].astype(F32)
        return own + self.pair[group, b].astype(F32)

    def to_line(self, i):
        grid, b = self.grid, pl.ds(*self.ranges[i])
        self.pair_copy[i].wait_recv()
        for d in (2, 1, 3):
            self.stage2[d, b] = self.chip_sum(grid.group_at(d), b).astype(BF16)
            self.line_copy[i][d - 1].start()

    def total(self, i):
        b = pl.ds(*self.ranges[i])
        total = self.chip_sum(self.grid.group, b)
        for d in range(1, DEPTH // 2):
            self.line_copy[i][d - 1].wait_recv()
            total = total + self.recv[d, b].astype(F32)
        return total

    def sent(self):
        for i in range(len(self.ranges)):
            self.sib_copy[i].wait_send()
            self.pair_copy[i].wait_send()
            for copy in self.line_copy[i]:
                copy.wait_send()


class RingGather:
    def __init__(self, grid, tiles, sems):
        a_s, a_r, b_s, b_r, c_s, c_r = sems
        self.strided, self.near, self.share = [], [], []
        for i, stage in enumerate(STAGES):
            b = pl.ds(STARTS[i], len(stage))
            own = tiles.at[b, grid.zhi, grid.par, grid.core, grid.rghi, grid.rglo]
            self.strided.append([
                remote(own, own, a_s.at[i, k], a_r.at[i, k], grid.on_ring(4 * k)) for k in (2, 1, 3)
            ])
            four = tiles.at[b, :, grid.par, grid.core, :, grid.rglo]
            self.near.append([
                remote(four, four, b_s.at[i, k], b_r.at[i, k], grid.on_ring(d)) for k, d in enumerate((2, 1, -1))
            ])
            all_mine = tiles.at[b, :, :, grid.core]
            self.share.append(remote(all_mine, all_mine, c_s.at[i], c_r.at[i], grid.sibling()))

    def begin(self, i):
        for copy in self.strided[i]:
            copy.start()

    def to_near(self, i):
        for copy in self.strided[i]:
            copy.wait_recv()
        for copy in self.near[i]:
            copy.start()

    def to_sibling(self, i):
        for copy in self.near[i]:
            copy.wait_recv()
        self.share[i].start()

    def arrived(self, i):
        self.share[i].wait_recv()

    def sent(self):
        for i in range(len(STAGES)):
            for copy in self.strided[i] + self.near[i]:
                copy.wait_send()
            self.share[i].wait_send()


def kernel(scale, cols, *refs):
    (
        key_ref, val_ref, cot_hbm, w_hbm, out_ref, grad_ref,
        w_ref, cot_ref, kmine, kother, kpair, vc, vc_in, call, pm, vm, ptotal,
        p0, p1, p2, p3, p4, p5, s0, s1, s2, s3, s4, s5, tiles, rall, dall, acc_f, acc_o, acc_b, comb, csend, osend, half,
        load_sem, swap_sem, wave0, wave1, wave2, wave3, c_send, c_recv,
        ps0, ps1, ps2, ps3, ps4, ps5, ss0, ss1, ss2, ss3, ss4, ss5, gs0, gs1, gs2, gs3, gs4, gs5,
        x_send, x_recv, f_send, f_recv, h_send, h_recv, o_send, o_recv,
    ) = refs
    grid = Grid()
    zhi, core, a = grid.zhi, grid.core, grid.a
    mb, width = key_ref.shape[1], key_ref.shape[2]
    rows = STEPS * mb

    loads = [pltpu.make_async_copy(w_hbm, w_ref, load_sem.at[0]), pltpu.make_async_copy(cot_hbm, cot_ref, load_sem.at[1])]
    for copy in loads:
        copy.start()
    targets = [grid.at_xy(*d) for d in XY] + [grid.sibling(), grid.pair()]
    targets += [grid.on_line(d) for d in range(1, DEPTH // 2)] + [grid.on_ring(d) for d in (4, 8, 12, 1, -1, -2)]
    targets += grid.sources()
    barrier = pltpu.get_barrier_semaphore()
    for device in targets:
        pl.semaphore_signal(barrier, inc=1, device_id=device, device_id_type=pl.DeviceIdType.MESH)

    kmine[:, a] = key_ref[...]
    key_rows = key_ref[...].reshape(rows, width)

    def padded(array):
        return jnp.concatenate([array, jnp.zeros(array.shape[:-1] + (LANES - cols,), array.dtype)], axis=-1)

    loads[0].wait()
    for zlo in range(DEPTH):
        block = jnp.dot(
            key_rows, w_ref[:, zlo * 4 * cols:(zlo + 1) * 4 * cols], preferred_element_type=F32
        )
        for c in range(2):
            for h in range(2):
                piece = padded(block[:, (2 * c + h) * cols:(2 * c + h + 1) * cols].astype(BF16))
                p0[zlo // 2, zlo % 2, c, pl.ds(h * (rows // TILE), rows // TILE)] = piece.reshape(-1, TILE, LANES)
    loads[1].wait()
    window = cot_ref[:, :, pl.ds(pl.multiple_of(grid.zlo * (4 * cols), LANES), 4 * cols)]
    window = jnp.where(core == 0, window[:, :, :2 * cols], window[:, :, 2 * cols:])
    for h in range(2):
        vc[h, 0] = padded(val_ref[:, :, h * cols:(h + 1) * cols])
        vc[h, 1] = padded(window[:, :, h * cols:(h + 1) * cols])
    pl.semaphore_wait(barrier, len(targets))

    def key_swap(s):
        return remote(key_ref.at[s], kpair.at[s], swap_sem.at[0, s], swap_sem.at[1, s], grid.partner())

    waves = (wave0, wave1, wave2, wave3)
    early = Wave(grid, kmine, waves, 0, 0, 3)
    late = Wave(grid, kmine, waves, 1, 1, 2)
    across = [Wave(grid, kother, waves, 2, 0, 3), Wave(grid, kother, waves, 3, 1, 2)]
    key_swaps = [key_swap(s) for s in range(STEPS)]
    vc_swap = remote(vc.at[1 - zhi], vc_in, swap_sem.at[0, STEPS], swap_sem.at[1, STEPS], grid.partner())
    psum = LineSum(grid, (p0, p1, p2, p3, p4, p5), (ps0, ps1, ps2, ps3, ps4, ps5), [(0, 2 * rows // TILE)])
    scores = LineSum(
        grid, (s0, s1, s2, s3, s4, s5), (ss0, ss1, ss2, ss3, ss4, ss5), [(STARTS[i], len(STAGES[i])) for i in range(4)]
    )
    ring = RingGather(grid, tiles, (gs0, gs1, gs2, gs3, gs4, gs5))

    early.start()
    key_swaps[3].start()
    key_swaps[1].start()
    psum.begin(0)
    psum.to_pair(0)
    early.forward()
    late.start()
    key_swaps[0].start()
    key_swaps[2].start()
    vc_swap.start()
    psum.to_line(0)

    def partial(stage):
        for t, s in STAGES[stage]:
            b = BLOCKS.index((t, s))
            left = jnp.concatenate(
                [jnp.where(zhi == 0, key_ref[t], kpair[t]), jnp.where(zhi == 0, kpair[t], key_ref[t])], axis=0
            )
            right = kmine[s].reshape(AREA * mb, width)
            block = lax.dot_general(left, right, (((1,), (1,)), ((), ())), preferred_element_type=F32).astype(BF16)
            for group in range(4):
                for q in range(4):
                    s0[group, q // 2, q % 2, b] = block[group * TILE:(group + 1) * TILE, q * LANES:(q + 1) * LANES]
        scores.begin(stage)

    def summed(stage):
        b = pl.ds(STARTS[stage], len(STAGES[stage]))
        tiles[b, zhi, grid.par, core, grid.rghi, grid.rglo] = scores.total(stage).astype(BF16)
        ring.begin(stage)

    def exchange(store, index, number, value):
        store[index, :, a] = value
        mine = store.at[index, :, a]
        copies = [
            remote(mine, mine, x_send.at[number, dy, dx], x_recv.at[number, dy, dx], grid.at_xy(dy, dx)) for dy, dx in XY
        ]
        for copy in copies:
            copy.start()
        return copies

    def received(copies):
        for copy in copies:
            copy.wait_recv()

    early.arrived()
    key_swaps[3].wait_recv()
    key_swaps[1].wait_recv()
    partial(0)
    scores.to_pair(0)
    late.forward()
    vc_swap.wait_recv()
    vm[zhi] = vc[zhi, 0]
    vm[1 - zhi] = vc_in[0]
    call[:, zhi, a] = vc[zhi, 1]
    call[:, 1 - zhi, a] = vc_in[1]
    own_c = call.at[:, :, a]
    spread = [remote(own_c, own_c, c_send.at[dy, dx], c_recv.at[dy, dx], grid.at_xy(dy, dx)) for dy, dx in XY]
    for copy in spread:
        copy.start()
    scores.to_line(0)

    ptotal[...] = psum.total(0).reshape(ptotal.shape)
    pm[zhi] = ptotal[zhi]
    p_swap = remote(ptotal.at[1 - zhi], pm.at[zhi], swap_sem.at[0, STEPS + 1], swap_sem.at[1, STEPS + 1], grid.partner())
    p_swap.start()

    summed(0)
    late.arrived()
    key_swaps[0].wait_recv()
    key_swaps[2].wait_recv()
    kother[:, a] = kpair[...]
    partial(1)
    scores.to_pair(1)
    partial(2)
    partial(3)
    ring.to_near(0)
    for wave in across:
        wave.start()
    scores.to_pair(2)
    scores.to_pair(3)
    scores.to_line(1)
    p_swap.wait_recv()

    acc_f[...] = jnp.zeros_like(acc_f)
    acc_o[...] = jnp.zeros_like(acc_o)
    acc_b[...] = jnp.zeros_like(acc_b)

    def tile_rows(t, s):
        b = BLOCKS.index((t, s))
        return jnp.concatenate(
            [tiles[b, h, p, c].reshape(4 * TILE, LANES) for h in range(2) for p in range(2) for c in range(2)], axis=1
        )

    def product(t, s, right):
        return jnp.dot(tile_rows(t, s), right.reshape(2 * AREA * mb, LANES), preferred_element_type=F32)

    def add_residual(t, s):
        term = product(t, s, rall[s])
        if t > s:
            acc_f[t] += (scale * momentum_sum(t - s)) * term
        acc_o[t] += (scale * momentum_sum(t + 1 - s)) * term

    def add_cotangent(s, t):
        acc_b[s] += (scale * momentum_sum(t + 1 - s)) * product(s, t, call[t])

    def add_adjoint(s, t):
        acc_b[s] += (scale * momentum_sum(t - s)) * product(s, t, dall[t])

    def projected(t):
        return pm[:, t].reshape(2 * mb, LANES)

    def residual(t):
        value = (projected(t) - acc_f[t] - vm[:, t].reshape(2 * mb, LANES).astype(F32)).astype(BF16)
        return exchange(rall, t, t, value.reshape(2, mb, LANES))

    def adjoint(s):
        value = (-acc_b[s]).astype(BF16).reshape(2, mb, LANES)
        copies = exchange(dall, s, STEPS + s, value) if s else []
        total = (value.astype(F32) + call[s, :, a].astype(F32)).astype(BF16)
        csend[s] = total
        x_hi, x_lo = lax.div(grid.x, 2), lax.rem(grid.x, 2)
        far = [
            remote(
                csend.at[s], comb.at[s, :, grid.y, x_hi, x_lo], f_send.at[s, k], f_recv.at[s, grid.y, x_lo], device
            )
            for k, device in enumerate(grid.owners())
        ]
        for copy in far:
            copy.start()
        return copies, far

    def gathered(s, far):
        for y in range(SIDE):
            for x in range(SIDE // 2):
                slot = comb.at[s, :, y, 1 - core, x]
                remote(csend.at[s], slot, f_send.at[s, 0], f_recv.at[s, y, x], grid.owners()[0]).wait_recv()
        held = comb.at[s, :, :, 1 - core]
        copy = remote(held, held, h_send.at[s], h_recv.at[s], grid.sibling())
        copy.start()
        return copy

    def gradient(s):
        total = None
        for blocks, which in ((kmine, zhi), (kother, 1 - zhi)):
            term = lax.dot_general(
                comb[s, which].reshape(AREA * mb, LANES), blocks[s].reshape(AREA * mb, width),
                (((0,), (0,)), ((), ())), preferred_element_type=F32,
            )
            total = term if total is None else total + term
        return total

    def output(t):
        osend[:, t] = (projected(t) - acc_o[t]).astype(BF16).reshape(2, mb, LANES)
        half[zhi, t] = osend[zhi, t]
        copy = remote(osend.at[1 - zhi, t], half.at[zhi, t], o_send.at[t], o_recv.at[t], grid.partner())
        copy.start()
        return copy

    r_copies, d_copies, far, shared, given = {}, {}, {}, {}, {}
    r_copies[0] = residual(0)
    scores.to_line(2)
    scores.to_line(3)
    ring.to_sibling(0)
    received(spread)
    summed(1)
    ring.arrived(0)

    add_cotangent(3, 3)
    d_copies[3], far[3] = adjoint(3)
    received(r_copies[0])
    add_residual(1, 0)
    r_copies[1] = residual(1)
    summed(2)
    for wave in across:
        wave.forward()
    ring.to_near(1)
    summed(3)
    ring.to_near(2)
    ring.to_sibling(1)
    ring.to_near(3)
    ring.arrived(1)
    add_cotangent(2, 2)
    add_cotangent(2, 3)
    add_residual(2, 0)

    received(d_copies[3])
    add_adjoint(2, 3)
    d_copies[2], far[2] = adjoint(2)
    received(r_copies[1])
    add_residual(2, 1)
    r_copies[2] = residual(2)
    ring.to_sibling(2)
    ring.arrived(2)
    for t in (1, 2, 3):
        add_cotangent(1, t)
    add_adjoint(1, 3)
    add_residual(3, 0)
    add_residual(3, 1)

    received(d_copies[2])
    add_adjoint(1, 2)
    d_copies[1], far[1] = adjoint(1)
    received(r_copies[2])
    add_residual(3, 2)
    r_copies[3] = residual(3)
    ring.to_sibling(3)
    ring.arrived(3)
    for t in range(STEPS):
        add_cotangent(0, t)
    add_adjoint(0, 3)
    add_adjoint(0, 2)

    received(d_copies[1])
    add_adjoint(0, 1)
    _, far[0] = adjoint(0)
    add_residual(0, 0)
    given[0] = output(0)
    add_residual(1, 1)
    given[1] = output(1)
    add_residual(2, 2)
    given[2] = output(2)
    received(r_copies[3])
    add_residual(3, 3)
    given[3] = output(3)
    for wave in across:
        wave.arrived()
    for s in (3, 2, 1):
        shared[s] = gathered(s, far[s])
    total = None
    for s in (3, 2, 1):
        shared[s].wait_recv()
        total = gradient(s) if total is None else total + gradient(s)
    shared[0] = gathered(0, far[0])
    shared[0].wait_recv()
    total = total + gradient(0)
    grad_ref[...] = total.T[:, :cols].astype(BF16)
    for t in range(STEPS):
        given[t].wait_recv()
        out_ref[t] = jnp.concatenate([half[0, t][:, :cols], half[1, t][:, :cols]], axis=-1)

    early.sent()
    late.sent()
    for wave in across:
        wave.sent()
    psum.sent()
    scores.sent()
    ring.sent()
    for copy in key_swaps + [vc_swap, p_swap] + spread + list(given.values()) + list(shared.values()):
        copy.wait_send()
    for group in list(r_copies.values()) + list(d_copies.values()) + list(far.values()):
        for copy in group:
            copy.wait_send()


def per_device(keys, values, cotangent, init_weight):
    steps, mb, width = keys.shape
    model_width = init_weight.shape[1]
    tok_count, tp_count = lax.axis_size("tok"), lax.axis_size("tp")
    cols = model_width // (2 * tp_count)
    hidden, batch_size = width * tp_count, mb * tok_count
    inner_rate = 0.5 * batch_size / (math.sqrt(hidden) + math.sqrt(batch_size)) ** 2
    scale = inner_rate / batch_size
    dma = pltpu.SemaphoreType.DMA
    rows = steps * mb
    blocks = 2 * rows // TILE

    def sums():
        return [
            pltpu.VMEM((4, 2, 2, blocks, TILE, LANES), BF16), pltpu.VMEM((4, 2, blocks, TILE, LANES), BF16),
        ] + [pltpu.VMEM((4, blocks, TILE, LANES), BF16)] * 4

    def sum_sems(count):
        return [dma((count,))] * 4 + [dma((count, 4))] * 2

    own = (steps, 2, AREA, mb, LANES)
    half = (2, steps, mb, LANES)
    scratch = [
        pltpu.VMEM(init_weight.shape, BF16), pltpu.VMEM(cotangent.shape, BF16),
        pltpu.VMEM((steps, AREA, mb, width), BF16), pltpu.VMEM((steps, AREA, mb, width), BF16),
        pltpu.VMEM(keys.shape, BF16),
        pltpu.VMEM((2, 2, steps, mb, LANES), BF16), pltpu.VMEM((2, steps, mb, LANES), BF16),
        pltpu.VMEM(own, BF16), pltpu.VMEM(half, F32), pltpu.VMEM(half, BF16), pltpu.VMEM(half, F32),
        *sums(), *sums(),
        pltpu.VMEM((16, 2, 2, 2, 2, 2, TILE, LANES), BF16),
        pltpu.VMEM(own, BF16), pltpu.VMEM(own, BF16),
        pltpu.VMEM((steps, 2 * mb, LANES), F32), pltpu.VMEM((steps, 2 * mb, LANES), F32),
        pltpu.VMEM((steps, 2 * mb, LANES), F32),
        pltpu.VMEM((steps, 2, SIDE, 2, SIDE // 2, mb, LANES), BF16), pltpu.VMEM((steps, 2, mb, LANES), BF16),
        pltpu.VMEM(half, BF16), pltpu.VMEM(half, BF16),
        dma((2,)), dma((2, steps + 2)),
        dma((4, 2, SIDE)), dma((4, 2, SIDE)), dma((4, 2, SIDE, SIDE)), dma((4, 2, SIDE, SIDE)),
        dma((SIDE, SIDE)), dma((SIDE, SIDE)),
        *sum_sems(1), *sum_sems(4),
        dma((4, 4)), dma((4, 4)), dma((4, 3)), dma((4, 3)), dma((4,)), dma((4,)),
        dma((2 * steps, SIDE, SIDE)), dma((2 * steps, SIDE, SIDE)),
        dma((steps, DEPTH)), dma((steps, SIDE, SIDE // 2)), dma((steps,)), dma((steps,)), dma((steps,)), dma((steps,)),
    ]
    vmem, hbm = pl.BlockSpec(memory_space=pltpu.VMEM), pl.BlockSpec(memory_space=pl.ANY)
    return pl.pallas_call(
        functools.partial(kernel, scale, cols),
        name="step",
        out_shape=[
            jax.ShapeDtypeStruct((steps, mb, 2 * cols), BF16), jax.ShapeDtypeStruct((width, cols), BF16),
        ],
        in_specs=[vmem, vmem, hbm, hbm],
        out_specs=[vmem, vmem],
        scratch_shapes=scratch,
        compiler_params=pltpu.CompilerParams(collective_id=0, has_side_effects=True, vmem_limit_bytes=VMEM_LIMIT),
    )(keys, values, cotangent, init_weight)


def solution(mesh):
    return jax.shard_map(
        per_device,
        mesh=mesh,
        in_specs=(P(None, "tok", "tp"), P(None, "tok", "tp"), P(None, "tok", None), P("tp", None)),
        out_specs=(P(None, "tok", "tp"), P("tp", "tok")),
        check_vma=False,
    )
```

```python
import functools
import math

import jax
import jax.numpy as jnp
from jax import lax
from jax.experimental import pallas as pl
from jax.experimental.pallas import tpu as pltpu
from jax.sharding import PartitionSpec as P

MOMENTUM = 0.9
LANES = 128
TILE = 16
F32 = jnp.float32
BF16 = jnp.bfloat16
VMEM_LIMIT = 56 * 1024 * 1024
STEPS = 4
SIDE = 4
DEPTH = 8
AREA = SIDE * SIDE
STAGES = (
    ((1, 0), (3, 3)),
    ((2, 0), (2, 1), (2, 2), (2, 3)),
    ((3, 0), (3, 1), (3, 2), (1, 1), (1, 2), (1, 3)),
    ((0, 0), (0, 1), (0, 2), (0, 3)),
)
BLOCKS = [block for stage in STAGES for block in stage]
STARTS = [sum(len(stage) for stage in STAGES[:i]) for i in range(len(STAGES))]


def momentum_sum(count):
    return (1.0 - MOMENTUM**count) / (1.0 - MOMENTUM)


class Grid:
    def __init__(self):
        tok, tp = lax.axis_index("tok"), lax.axis_index("tp")
        self.tok, self.tp = tok, tp
        self.y = lax.div(tok, 2 * SIDE)
        self.zhi = lax.rem(lax.div(tok, SIDE), 2)
        self.x = lax.rem(tok, SIDE)
        self.zlo = lax.div(tp, 2)
        self.core = lax.rem(tp, 2)
        self.a = self.y * SIDE + self.x
        self.z = self.zhi * DEPTH + self.zlo
        self.group = lax.div(self.zlo, 2)
        self.par = lax.rem(self.zlo, 2)
        self.rghi = lax.div(self.zlo, 4)
        self.rglo = lax.rem(self.group, 2)

    def tok_of(self, y, zhi, x):
        return y * (2 * SIDE) + zhi * SIDE + x

    def at_xy(self, dy, dx):
        y = lax.rem(self.y + dy + SIDE, SIDE)
        x = lax.rem(self.x + dx + SIDE, SIDE)
        return (self.tok_of(y, self.zhi, x), self.tp)

    def a_at(self, dy, dx):
        y = lax.rem(self.y + dy + SIDE, SIDE)
        x = lax.rem(self.x + dx + SIDE, SIDE)
        return y * SIDE + x

    def partner(self):
        return (self.tok_of(self.y, 1 - self.zhi, self.x), self.tp)

    def sibling(self):
        return (self.tok, self.zlo * 2 + 1 - self.core)

    def pair(self):
        return (self.tok, (self.zlo + 1 - 2 * self.par) * 2 + self.core)

    def group_at(self, d):
        return lax.rem(self.group + d + DEPTH // 2, DEPTH // 2)

    def on_line(self, d):
        return (self.tok, (self.group_at(d) * 2 + self.par) * 2 + self.core)

    def on_ring(self, d):
        z = lax.rem(self.z + d + 2 * DEPTH, 2 * DEPTH)
        zhi, zlo = lax.div(z, DEPTH), lax.rem(z, DEPTH)
        return (self.tok_of(self.y, zhi, self.x), zlo * 2 + self.core)

    def owners(self):
        core = 1 - lax.div(self.x, 2)
        return [(2 * self.tp + self.zhi, lax.rem(self.zlo + k, DEPTH) * 2 + core) for k in range(DEPTH)]

    def sources(self):
        tp, zhi = lax.div(self.tok, 2), lax.rem(self.tok, 2)
        return [
            (self.tok_of(y, zhi, (1 - self.core) * 2 + x), tp) for y in range(SIDE) for x in range(SIDE // 2)
        ]


XY = [(dy, dx) for dy in range(SIDE) for dx in range(SIDE) if (dy, dx) != (0, 0)]


def remote(src, dst, send, recv, device):
    return pltpu.make_async_remote_copy(
        src_ref=src, dst_ref=dst, send_sem=send, recv_sem=recv, device_id=device, device_id_type=pl.DeviceIdType.MESH
    )


def await_recv(like, sem):
    pltpu.make_async_copy(like, like, sem).wait()


class Wave:
    def __init__(self, grid, blocks, sems, number, first, second):
        self.first, self.own, self.rest, self.blocks = [], [], [[], []], blocks
        send, recv1, recv2 = [sem.at[number] for sem in sems]
        self.send, self.recv1, self.recv2 = send, recv1, recv2
        for h, s in enumerate((first, second)):
            for d in range(1, SIDE):
                mine = blocks.at[s, grid.a]
                peer = grid.at_xy(d, 0) if h == 0 else grid.at_xy(0, d)
                self.first.append(remote(mine, mine, send, recv1.at[h], peer))
            for d in range(SIDE):
                held = blocks.at[s, grid.a_at(-d, 0) if h == 0 else grid.a_at(0, -d)]
                for e in range(1, SIDE):
                    peer = grid.at_xy(0, e) if h == 0 else grid.at_xy(e, 0)
                    copy = remote(held, held, send, recv2, peer)
                    (self.rest[h] if d else self.own).append(copy)

    def start(self):
        for copy in self.first:
            copy.start()

    def start_own(self):
        for copy in self.own:
            copy.start()

    def forward(self):
        for h in range(2):
            await_recv(self.blocks.at[0, pl.ds(0, SIDE - 1)], self.recv1.at[h])
            for copy in self.rest[h]:
                copy.start()

    def arrived(self):
        await_recv(self.blocks.at[pl.ds(0, 2), pl.ds(0, SIDE * (SIDE - 1))], self.recv2)

    def sent(self):
        await_recv(self.blocks.at[pl.ds(0, 2), pl.ds(0, (SIDE + 1) * (SIDE - 1))], self.send)


class LineSum:
    def __init__(self, grid, bufs, sems, ranges):
        self.grid, self.ranges = grid, ranges
        self.part, self.sib, self.stage1, self.pair, self.stage2, self.recv = bufs
        sib_s, sib_r, pair_s, pair_r, line_s, line_r = sems
        self.sib_copy, self.pair_copy, self.line_copy = [], [], []
        self.line_s, self.line_r = line_s, line_r
        for i, (start, size) in enumerate(ranges):
            b = pl.ds(start, size)
            self.sib_copy.append(remote(
                self.part.at[:, :, 1 - grid.core, b], self.sib.at[:, :, b], sib_s.at[i], sib_r.at[i], grid.sibling()
            ))
            self.pair_copy.append(remote(
                self.stage1.at[:, b], self.pair.at[:, b], pair_s.at[i], pair_r.at[i], grid.pair()
            ))
            self.line_copy.append([
                remote(self.stage2.at[d, b], self.recv.at[d, b], line_s.at[i], line_r.at[i], grid.on_line(d))
                for d in range(1, DEPTH // 2)
            ])

    def begin(self, i):
        self.sib_copy[i].start()

    def to_pair(self, i):
        grid, b = self.grid, pl.ds(*self.ranges[i])
        self.sib_copy[i].wait_recv()
        other = 1 - grid.par
        own = self.part[:, other, grid.core, b].astype(F32) + self.sib[:, other, b].astype(F32)
        self.stage1[:, b] = own.astype(BF16)
        self.pair_copy[i].start()

    def chip_sum(self, group, b):
        grid = self.grid
        own = self.part[group, grid.par, grid.core, b].astype(F32) + self.sib[group, grid.par, b].astype(F32)
        return own + self.pair[group, b].astype(F32)

    def to_line(self, i):
        grid, b = self.grid, pl.ds(*self.ranges[i])
        self.pair_copy[i].wait_recv()
        for d in (2, 1, 3):
            self.stage2[d, b] = self.chip_sum(grid.group_at(d), b).astype(BF16)
            self.line_copy[i][d - 1].start()

    def total(self, i):
        b = pl.ds(*self.ranges[i])
        total = self.chip_sum(self.grid.group, b)
        await_recv(self.recv.at[pl.ds(1, DEPTH // 2 - 1), b], self.line_r.at[i])
        for d in range(1, DEPTH // 2):
            total = total + self.recv[d, b].astype(F32)
        return total

    def sent(self):
        for i in range(len(self.ranges)):
            self.sib_copy[i].wait_send()
            self.pair_copy[i].wait_send()
            await_recv(self.stage2.at[pl.ds(1, DEPTH // 2 - 1), pl.ds(*self.ranges[i])], self.line_s.at[i])


class RingGather:
    def __init__(self, grid, tiles, sems):
        a_s, a_r, b_s, b_r, c_s, c_r = sems
        self.tiles, self.sems = tiles, sems
        self.strided, self.near, self.share = [], [], []
        for i, stage in enumerate(STAGES):
            b = pl.ds(STARTS[i], len(stage))
            own = tiles.at[b, grid.zhi, grid.par, grid.core, grid.rghi, grid.rglo]
            self.strided.append([
                remote(own, own, a_s.at[i], a_r.at[i], grid.on_ring(4 * k)) for k in (2, 1, 3)
            ])
            four = tiles.at[b, :, grid.par, grid.core, :, grid.rglo]
            self.near.append([
                remote(four, four, b_s.at[i], b_r.at[i], grid.on_ring(d)) for d in (2, 1, -1)
            ])
            all_mine = tiles.at[b, :, :, grid.core]
            self.share.append(remote(all_mine, all_mine, c_s.at[i], c_r.at[i], grid.sibling()))

    def like(self, i, near):
        count = pl.ds(0, 3 * len(STAGES[i]) // 2)
        return self.tiles.at[count, 0, 0] if near else self.tiles.at[count, 0, 0, 0, 0]

    def begin(self, i):
        for copy in self.strided[i]:
            copy.start()

    def to_near(self, i):
        await_recv(self.like(i, False), self.sems[1].at[i])
        for copy in self.near[i]:
            copy.start()

    def to_sibling(self, i):
        await_recv(self.like(i, True), self.sems[3].at[i])
        self.share[i].start()

    def arrived(self, i):
        self.share[i].wait_recv()

    def sent(self):
        for i in range(len(STAGES)):
            await_recv(self.like(i, False), self.sems[0].at[i])
            await_recv(self.like(i, True), self.sems[2].at[i])
            self.share[i].wait_send()


def kernel(scale, cols, *refs):
    (
        key_ref, val_ref, cot_hbm, w_hbm, out_ref, grad_ref,
        w_ref, cot_ref, kmine, kother, kpair, vc, vc_in, call, pm, vm, ptotal,
        p0, p1, p2, p3, p4, p5, s0, s1, s2, s3, s4, s5, tiles, rall, dall, acc_f, acc_o, acc_b, comb, csend, osend, half,
        load_sem, swap_sem, wave0, wave1, wave2, c_send, c_recv,
        ps0, ps1, ps2, ps3, ps4, ps5, ss0, ss1, ss2, ss3, ss4, ss5, gs0, gs1, gs2, gs3, gs4, gs5,
        x_send, x_recv, f_send, f_recv, h_send, h_recv, o_send, o_recv,
    ) = refs
    grid = Grid()
    zhi, core, a = grid.zhi, grid.core, grid.a
    mb, width = key_ref.shape[1], key_ref.shape[2]
    rows = STEPS * mb

    loads = [pltpu.make_async_copy(w_hbm, w_ref, load_sem.at[0]), pltpu.make_async_copy(cot_hbm, cot_ref, load_sem.at[1])]
    for copy in loads:
        copy.start()
    targets = [grid.at_xy(*d) for d in XY] + [grid.sibling(), grid.pair()]
    targets += [grid.on_line(d) for d in range(1, DEPTH // 2)] + [grid.on_ring(d) for d in (4, 8, 12, 1, -1, -2)]
    targets += grid.sources()
    barrier = pltpu.get_barrier_semaphore()
    for device in targets:
        pl.semaphore_signal(barrier, inc=1, device_id=device, device_id_type=pl.DeviceIdType.MESH)

    kmine[:, a] = key_ref[...]
    key_rows = key_ref[...].reshape(rows, width)

    def padded(array):
        return jnp.concatenate([array, jnp.zeros(array.shape[:-1] + (LANES - cols,), array.dtype)], axis=-1)

    loads[0].wait()
    for zlo in range(DEPTH):
        block = jnp.dot(
            key_rows, w_ref[:, zlo * 4 * cols:(zlo + 1) * 4 * cols], preferred_element_type=F32
        )
        for c in range(2):
            for h in range(2):
                piece = padded(block[:, (2 * c + h) * cols:(2 * c + h + 1) * cols].astype(BF16))
                p0[zlo // 2, zlo % 2, c, pl.ds(h * (rows // TILE), rows // TILE)] = piece.reshape(-1, TILE, LANES)
    loads[1].wait()
    window = cot_ref[:, :, pl.ds(pl.multiple_of(grid.zlo * (4 * cols), LANES), 4 * cols)]
    window = jnp.where(core == 0, window[:, :, :2 * cols], window[:, :, 2 * cols:])
    for h in range(2):
        vc[h, 0] = padded(val_ref[:, :, h * cols:(h + 1) * cols])
        vc[h, 1] = padded(window[:, :, h * cols:(h + 1) * cols])
    pl.semaphore_wait(barrier, len(targets))

    def key_swap(s):
        return remote(key_ref.at[s], kpair.at[s], swap_sem.at[0, s], swap_sem.at[1, s], grid.partner())

    waves = (wave0, wave1, wave2)
    early = Wave(grid, kmine, waves, 0, 0, 3)
    late = Wave(grid, kmine, waves, 1, 1, 2)
    across = [Wave(grid, kother, waves, 2, 0, 3), Wave(grid, kother, waves, 3, 1, 2)]
    key_swaps = [key_swap(s) for s in range(STEPS)]
    vc_swap = remote(vc.at[1 - zhi], vc_in, swap_sem.at[0, STEPS], swap_sem.at[1, STEPS], grid.partner())
    psum = LineSum(grid, (p0, p1, p2, p3, p4, p5), (ps0, ps1, ps2, ps3, ps4, ps5), [(0, 2 * rows // TILE)])
    scores = LineSum(
        grid, (s0, s1, s2, s3, s4, s5), (ss0, ss1, ss2, ss3, ss4, ss5), [(STARTS[i], len(STAGES[i])) for i in range(4)]
    )
    ring = RingGather(grid, tiles, (gs0, gs1, gs2, gs3, gs4, gs5))

    def partial(stage):
        for t, s in STAGES[stage]:
            b = BLOCKS.index((t, s))
            left = jnp.concatenate(
                [jnp.where(zhi == 0, key_ref[t], kpair[t]), jnp.where(zhi == 0, kpair[t], key_ref[t])], axis=0
            )
            right = kmine[s].reshape(AREA * mb, width)
            block = lax.dot_general(left, right, (((1,), (1,)), ((), ())), preferred_element_type=F32).astype(BF16)
            for group in range(4):
                for q in range(4):
                    s0[group, q // 2, q % 2, b] = block[group * TILE:(group + 1) * TILE, q * LANES:(q + 1) * LANES]
        scores.begin(stage)

    def summed(stage):
        b = pl.ds(STARTS[stage], len(STAGES[stage]))
        tiles[b, zhi, grid.par, core, grid.rghi, grid.rglo] = scores.total(stage).astype(BF16)
        ring.begin(stage)

    def exchange(store, index, number, value):
        store[index, :, a] = value
        mine = store.at[index, :, a]
        copies = [
            remote(mine, mine, x_send.at[number], x_recv.at[number], grid.at_xy(dy, dx)) for dy, dx in XY
        ]
        for copy in copies:
            copy.start()
        return store.at[index, :, pl.ds(0, AREA - 1)], number

    def received(sent):
        await_recv(sent[0], x_recv.at[sent[1]])

    acc_f[...] = jnp.zeros_like(acc_f)
    acc_o[...] = jnp.zeros_like(acc_o)
    acc_b[...] = jnp.zeros_like(acc_b)

    def tile_rows(t, s):
        b = BLOCKS.index((t, s))
        return jnp.concatenate(
            [tiles[b, h, p, c].reshape(4 * TILE, LANES) for h in range(2) for p in range(2) for c in range(2)], axis=1
        )

    def product(t, s, right):
        return jnp.dot(tile_rows(t, s), right.reshape(2 * AREA * mb, LANES), preferred_element_type=F32)

    def add_residual(t, s):
        term = product(t, s, rall[s])
        if t > s:
            acc_f[t] += (scale * momentum_sum(t - s)) * term
        acc_o[t] += (scale * momentum_sum(t + 1 - s)) * term

    def add_cotangent(s, t):
        acc_b[s] += (scale * momentum_sum(t + 1 - s)) * product(s, t, call[t])

    def add_adjoint(s, t):
        acc_b[s] += (scale * momentum_sum(t - s)) * product(s, t, dall[t])

    def projected(t):
        return pm[:, t].reshape(2 * mb, LANES).astype(F32)

    def residual(t):
        value = (projected(t) - acc_f[t] - vm[:, t].reshape(2 * mb, LANES).astype(F32)).astype(BF16)
        return exchange(rall, t, t, value.reshape(2, mb, LANES))

    def adjoint(s):
        value = (-acc_b[s]).astype(BF16).reshape(2, mb, LANES)
        copies = exchange(dall, s, STEPS + s, value) if s else None
        total = (value.astype(F32) + call[s, :, a].astype(F32)).astype(BF16)
        csend[s] = total
        x_hi, x_lo = lax.div(grid.x, 2), lax.rem(grid.x, 2)
        far = [
            remote(
                csend.at[s], comb.at[s, :, grid.y, x_hi, x_lo], f_send.at[s], f_recv.at[s], device
            )
            for device in grid.owners()
        ]
        for copy in far:
            copy.start()
        return copies

    def gathered(s):
        held = comb.at[s, :, :, 1 - core]
        await_recv(held, f_recv.at[s])
        copy = remote(held, held, h_send.at[s], h_recv.at[s], grid.sibling())
        copy.start()
        return copy

    def gradient(s):
        total = None
        for blocks, which in ((kmine, zhi), (kother, 1 - zhi)):
            term = lax.dot_general(
                comb[s, which].reshape(AREA * mb, LANES), blocks[s].reshape(AREA * mb, width),
                (((0,), (0,)), ((), ())), preferred_element_type=F32,
            )
            total = term if total is None else total + term
        return total

    def output(t):
        osend[:, t] = (projected(t) - acc_o[t]).astype(BF16).reshape(2, mb, LANES)
        half[zhi, t] = osend[zhi, t]
        copy = remote(osend.at[1 - zhi, t], half.at[zhi, t], o_send.at[t], o_recv.at[t], grid.partner())
        copy.start()
        return copy

    r_copies, d_copies, shared, given = {}, {}, {}, {}

    early.start()
    key_swaps[3].start()
    key_swaps[1].start()
    early.start_own()
    psum.begin(0)
    late.start()
    key_swaps[2].start()
    key_swaps[0].start()
    psum.to_pair(0)
    early.forward()
    late.start_own()
    late.forward()
    vc_swap.start()
    early.arrived()
    key_swaps[3].wait_recv()
    key_swaps[1].wait_recv()
    partial(0)
    psum.to_line(0)
    scores.to_pair(0)
    late.arrived()
    key_swaps[2].wait_recv()
    key_swaps[0].wait_recv()
    partial(1)
    scores.to_line(0)
    scores.to_pair(1)
    partial(2)
    partial(3)
    vc_swap.wait_recv()
    vm[zhi] = vc[zhi, 0]
    vm[1 - zhi] = vc_in[0]
    call[:, zhi, a] = vc[zhi, 1]
    call[:, 1 - zhi, a] = vc_in[1]
    own_c = (call.at[pl.ds(3, 1), :, a], call.at[pl.ds(0, 3), :, a])
    spread = [
        remote(own_c[k], own_c[k], c_send.at[k], c_recv.at[k], grid.at_xy(dy, dx)) for k in range(2) for dy, dx in XY
    ]
    all_c = (call.at[pl.ds(3, 1), :, pl.ds(0, AREA - 1)], call.at[pl.ds(0, 3), :, pl.ds(0, AREA - 1)])
    for copy in spread:
        copy.start()
    summed(0)
    scores.to_line(1)
    ptotal[...] = psum.total(0).reshape(ptotal.shape).astype(BF16)
    pm[zhi] = ptotal[zhi]
    p_swap = remote(ptotal.at[1 - zhi], pm.at[zhi], swap_sem.at[0, STEPS + 1], swap_sem.at[1, STEPS + 1], grid.partner())
    p_swap.start()
    scores.to_pair(2)
    scores.to_pair(3)
    kother[:, a] = kpair[...]
    ring.to_near(0)
    for wave in across:
        wave.start()
        wave.start_own()
    summed(1)
    p_swap.wait_recv()
    r_copies[0] = residual(0)
    ring.to_sibling(0)
    scores.to_line(2)
    scores.to_line(3)
    await_recv(all_c[0], c_recv.at[0])
    ring.arrived(0)

    add_cotangent(3, 3)
    d_copies[3] = adjoint(3)
    received(r_copies[0])
    add_residual(1, 0)
    r_copies[1] = residual(1)
    ring.to_near(1)
    summed(2)
    for wave in across:
        wave.forward()
    ring.to_sibling(1)
    await_recv(all_c[1], c_recv.at[1])
    ring.arrived(1)
    add_cotangent(2, 2)
    add_cotangent(2, 3)
    add_residual(2, 0)

    received(d_copies[3])
    add_adjoint(2, 3)
    d_copies[2] = adjoint(2)
    received(r_copies[1])
    add_residual(2, 1)
    r_copies[2] = residual(2)
    ring.to_near(2)
    summed(3)
    ring.to_sibling(2)
    ring.arrived(2)
    for t in (1, 2, 3):
        add_cotangent(1, t)
    add_adjoint(1, 3)
    add_residual(3, 0)
    add_residual(3, 1)

    received(d_copies[2])
    add_adjoint(1, 2)
    d_copies[1] = adjoint(1)
    received(r_copies[2])
    add_residual(3, 2)
    r_copies[3] = residual(3)
    ring.to_near(3)
    ring.to_sibling(3)
    ring.arrived(3)
    for t in range(STEPS):
        add_cotangent(0, t)
    add_adjoint(0, 3)
    add_adjoint(0, 2)

    received(d_copies[1])
    add_adjoint(0, 1)
    adjoint(0)
    add_residual(0, 0)
    given[0] = output(0)
    add_residual(1, 1)
    given[1] = output(1)
    add_residual(2, 2)
    given[2] = output(2)
    received(r_copies[3])
    add_residual(3, 3)
    given[3] = output(3)
    for wave in across:
        wave.arrived()
    for s in (3, 2, 1):
        shared[s] = gathered(s)
    total = None
    for s in (3, 2, 1):
        shared[s].wait_recv()
        total = gradient(s) if total is None else total + gradient(s)
    shared[0] = gathered(0)
    shared[0].wait_recv()
    total = total + gradient(0)
    grad_ref[...] = total[:cols].astype(BF16)
    for t in range(STEPS):
        given[t].wait_recv()
        out_ref[t] = jnp.concatenate([half[0, t][:, :cols], half[1, t][:, :cols]], axis=-1)

    early.sent()
    late.sent()
    for wave in across:
        wave.sent()
    psum.sent()
    scores.sent()
    ring.sent()
    for copy in key_swaps + [vc_swap, p_swap] + list(given.values()) + list(shared.values()):
        copy.wait_send()
    for k in range(2):
        await_recv(all_c[k], c_send.at[k])
    for like, number in list(r_copies.values()) + list(d_copies.values()):
        await_recv(like, x_send.at[number])
    for s in range(STEPS):
        await_recv(comb.at[s, :, :, 1 - core], f_send.at[s])


def per_device(keys, values, cotangent, init_weight):
    steps, mb, width = keys.shape
    model_width = init_weight.shape[1]
    tok_count, tp_count = lax.axis_size("tok"), lax.axis_size("tp")
    cols = model_width // (2 * tp_count)
    hidden, batch_size = width * tp_count, mb * tok_count
    inner_rate = 0.5 * batch_size / (math.sqrt(hidden) + math.sqrt(batch_size)) ** 2
    scale = inner_rate / batch_size
    dma = pltpu.SemaphoreType.DMA
    rows = steps * mb
    blocks = 2 * rows // TILE

    def sums():
        return [
            pltpu.VMEM((4, 2, 2, blocks, TILE, LANES), BF16), pltpu.VMEM((4, 2, blocks, TILE, LANES), BF16),
        ] + [pltpu.VMEM((4, blocks, TILE, LANES), BF16)] * 4

    def sum_sems(count):
        return [dma((count,))] * 6

    own = (steps, 2, AREA, mb, LANES)
    half = (2, steps, mb, LANES)
    scratch = [
        pltpu.VMEM(init_weight.shape, BF16), pltpu.VMEM(cotangent.shape, BF16),
        pltpu.VMEM((steps, AREA, mb, width), BF16), pltpu.VMEM((steps, AREA, mb, width), BF16),
        pltpu.VMEM(keys.shape, BF16),
        pltpu.VMEM((2, 2, steps, mb, LANES), BF16), pltpu.VMEM((2, steps, mb, LANES), BF16),
        pltpu.VMEM(own, BF16), pltpu.VMEM(half, BF16), pltpu.VMEM(half, BF16), pltpu.VMEM(half, BF16),
        *sums(), *sums(),
        pltpu.VMEM((16, 2, 2, 2, 2, 2, TILE, LANES), BF16),
        pltpu.VMEM(own, BF16), pltpu.VMEM(own, BF16),
        pltpu.VMEM((steps, 2 * mb, LANES), F32), pltpu.VMEM((steps, 2 * mb, LANES), F32),
        pltpu.VMEM((steps, 2 * mb, LANES), F32),
        pltpu.VMEM((steps, 2, SIDE, 2, SIDE // 2, mb, LANES), BF16), pltpu.VMEM((steps, 2, mb, LANES), BF16),
        pltpu.VMEM(half, BF16), pltpu.VMEM(half, BF16),
        dma((2,)), dma((2, steps + 2)),
        dma((4,)), dma((4, 2)), dma((4,)), dma((2,)), dma((2,)),
        *sum_sems(1), *sum_sems(4),
        *[dma((4,))] * 6,
        dma((2 * steps,)), dma((2 * steps,)),
        *[dma((steps,))] * 6,
    ]
    vmem, hbm = pl.BlockSpec(memory_space=pltpu.VMEM), pl.BlockSpec(memory_space=pl.ANY)
    out, grad = pl.pallas_call(
        functools.partial(kernel, scale, cols),
        name="step",
        out_shape=[
            jax.ShapeDtypeStruct((steps, mb, 2 * cols), BF16), jax.ShapeDtypeStruct((cols, width), BF16),
        ],
        in_specs=[vmem, vmem, hbm, hbm],
        out_specs=[vmem, vmem],
        scratch_shapes=scratch,
        compiler_params=pltpu.CompilerParams(collective_id=0, has_side_effects=True, vmem_limit_bytes=VMEM_LIMIT),
    )(keys, values, cotangent, init_weight)
    return out, grad.T


def solution(mesh):
    return jax.shard_map(
        per_device,
        mesh=mesh,
        in_specs=(P(None, "tok", "tp"), P(None, "tok", "tp"), P(None, "tok", None), P("tp", None)),
        out_specs=(P(None, "tok", "tp"), P("tp", "tok")),
        check_vma=False,
    )
```

```python
import functools
import math

import jax
import jax.numpy as jnp
from jax import lax
from jax.experimental import pallas as pl
from jax.experimental.pallas import tpu as pltpu
from jax.sharding import PartitionSpec as P

MOMENTUM = 0.9
LANES = 128
TILE = 16
F32 = jnp.float32
BF16 = jnp.bfloat16
VMEM_LIMIT = 56 * 1024 * 1024
STEPS = 4
SIDE = 4
DEPTH = 8
AREA = SIDE * SIDE
STAGES = (
    ((1, 0), (3, 3), (2, 0), (2, 1), (2, 2), (2, 3)),
    ((3, 0), (3, 1), (3, 2), (1, 1), (1, 2), (1, 3)),
    ((0, 0), (0, 1), (0, 2), (0, 3)),
)
BLOCKS = [block for stage in STAGES for block in stage]
STARTS = [sum(len(stage) for stage in STAGES[:i]) for i in range(len(STAGES))]


def momentum_sum(count):
    return (1.0 - MOMENTUM**count) / (1.0 - MOMENTUM)


class Grid:
    def __init__(self):
        tok, tp = lax.axis_index("tok"), lax.axis_index("tp")
        self.tok, self.tp = tok, tp
        self.y = lax.div(tok, 2 * SIDE)
        self.zhi = lax.rem(lax.div(tok, SIDE), 2)
        self.x = lax.rem(tok, SIDE)
        self.zlo = lax.div(tp, 2)
        self.core = lax.rem(tp, 2)
        self.a = self.y * SIDE + self.x
        self.z = self.zhi * DEPTH + self.zlo
        self.group = lax.div(self.zlo, 2)
        self.par = lax.rem(self.zlo, 2)
        self.rghi = lax.div(self.zlo, 4)
        self.rglo = lax.rem(self.group, 2)

    def tok_of(self, y, zhi, x):
        return y * (2 * SIDE) + zhi * SIDE + x

    def at_xy(self, dy, dx):
        y = lax.rem(self.y + dy + SIDE, SIDE)
        x = lax.rem(self.x + dx + SIDE, SIDE)
        return (self.tok_of(y, self.zhi, x), self.tp)

    def a_at(self, dy, dx):
        y = lax.rem(self.y + dy + SIDE, SIDE)
        x = lax.rem(self.x + dx + SIDE, SIDE)
        return y * SIDE + x

    def partner(self):
        return (self.tok_of(self.y, 1 - self.zhi, self.x), self.tp)

    def sibling(self):
        return (self.tok, self.zlo * 2 + 1 - self.core)

    def pair(self):
        return (self.tok, (self.zlo + 1 - 2 * self.par) * 2 + self.core)

    def group_at(self, d):
        return lax.rem(self.group + d + DEPTH // 2, DEPTH // 2)

    def on_line(self, d):
        return (self.tok, (self.group_at(d) * 2 + self.par) * 2 + self.core)

    def on_ring(self, d):
        z = lax.rem(self.z + d + 2 * DEPTH, 2 * DEPTH)
        zhi, zlo = lax.div(z, DEPTH), lax.rem(z, DEPTH)
        return (self.tok_of(self.y, zhi, self.x), zlo * 2 + self.core)

    def owner(self, k):
        zlo = lax.rem(self.group + k, DEPTH // 2) * 2 + lax.rem(self.x, 2)
        return (2 * self.tp + self.zhi, zlo * 2 + 1 - lax.div(self.x, 2))

    def sources(self):
        tp, zhi = lax.div(self.tok, 2), lax.rem(self.tok, 2)
        return [(self.tok_of(y, zhi, (1 - self.core) * 2 + self.par), tp) for y in range(SIDE)]


XY = [(dy, dx) for dy in range(SIDE) for dx in range(SIDE) if (dy, dx) != (0, 0)]


def remote(src, dst, send, recv, device):
    return pltpu.make_async_remote_copy(
        src_ref=src, dst_ref=dst, send_sem=send, recv_sem=recv, device_id=device, device_id_type=pl.DeviceIdType.MESH
    )


def repeat(first, stop, body):
    def step(i, carry):
        body(i)
        return carry

    lax.fori_loop(first, stop, step, 0)


def await_recv(like, sem):
    pltpu.make_async_copy(like, like, sem).wait()


class Wave:
    def __init__(self, grid, blocks, sems, number, first, second):
        self.grid, self.blocks, self.steps = grid, blocks, (first, second)
        self.send, self.recv1, self.recv2 = [sem.at[number] for sem in sems]

    def along(self, h, d):
        return (d, 0) if h == 0 else (0, d)

    def start(self):
        def body(d):
            for h in range(2):
                mine = self.blocks.at[self.steps[h], self.grid.a]
                remote(mine, mine, self.send, self.recv1.at[h], self.grid.at_xy(*self.along(h, d))).start()

        repeat(1, SIDE, body)

    def pass_on(self, h, d, e):
        held = self.blocks.at[self.steps[h], self.grid.a_at(*self.along(h, -d))]
        remote(held, held, self.send, self.recv2, self.grid.at_xy(*self.along(1 - h, e))).start()

    def start_own(self):
        def body(e):
            for h in range(2):
                self.pass_on(h, 0, e)

        repeat(1, SIDE, body)

    def forward(self):
        for h in range(2):
            await_recv(self.blocks.at[0, pl.ds(0, SIDE - 1)], self.recv1.at[h])
            count = SIDE - 1
            repeat(0, count * count, lambda k, h=h: self.pass_on(h, lax.div(k, count) + 1, lax.rem(k, count) + 1))

    def arrived(self):
        await_recv(self.blocks.at[pl.ds(0, 2), pl.ds(0, SIDE * (SIDE - 1))], self.recv2)

    def sent(self):
        await_recv(self.blocks.at[pl.ds(0, 2), pl.ds(0, (SIDE + 1) * (SIDE - 1))], self.send)


class LineSum:
    def __init__(self, grid, bufs, sems, ranges):
        self.grid, self.ranges = grid, ranges
        self.part, self.sib, self.stage1, self.pair, self.stage2, self.recv = bufs
        sib_s, sib_r, pair_s, pair_r, line_s, line_r = sems
        self.sib_copy, self.pair_copy = [], []
        self.line_s, self.line_r = line_s, line_r
        for i, (start, size) in enumerate(ranges):
            b = pl.ds(start, size)
            self.sib_copy.append(remote(
                self.part.at[:, :, 1 - grid.core, b], self.sib.at[:, :, b], sib_s.at[i], sib_r.at[i], grid.sibling()
            ))
            self.pair_copy.append(remote(
                self.stage1.at[:, b], self.pair.at[:, b], pair_s.at[i], pair_r.at[i], grid.pair()
            ))

    def begin(self, i):
        self.sib_copy[i].start()

    def to_pair(self, i):
        grid, b = self.grid, pl.ds(*self.ranges[i])
        self.sib_copy[i].wait_recv()
        other = 1 - grid.par

        def body(group):
            own = self.part[group, other, grid.core, b].astype(F32) + self.sib[group, other, b].astype(F32)
            self.stage1[group, b] = own.astype(BF16)

        repeat(0, DEPTH // 2, body)
        self.pair_copy[i].start()

    def chip_sum(self, group, b):
        grid = self.grid
        own = self.part[group, grid.par, grid.core, b].astype(F32) + self.sib[group, grid.par, b].astype(F32)
        return own + self.pair[group, b].astype(F32)

    def to_line(self, i):
        grid, b = self.grid, pl.ds(*self.ranges[i])
        self.pair_copy[i].wait_recv()

        def body(d):
            self.stage2[d, b] = self.chip_sum(grid.group_at(d), b).astype(BF16)
            remote(self.stage2.at[d, b], self.recv.at[d, b], self.line_s.at[i], self.line_r.at[i], grid.on_line(d)).start()

        repeat(1, DEPTH // 2, body)

    def total(self, i):
        b = pl.ds(*self.ranges[i])
        total = self.chip_sum(self.grid.group, b)
        await_recv(self.recv.at[pl.ds(1, DEPTH // 2 - 1), b], self.line_r.at[i])
        for d in range(1, DEPTH // 2):
            total = total + self.recv[d, b].astype(F32)
        return total

    def sent(self):
        for i in range(len(self.ranges)):
            self.sib_copy[i].wait_send()
            self.pair_copy[i].wait_send()
            await_recv(self.stage2.at[pl.ds(1, DEPTH // 2 - 1), pl.ds(*self.ranges[i])], self.line_s.at[i])


class RingGather:
    def __init__(self, grid, tiles, sems):
        a_s, a_r, b_s, b_r, c_s, c_r = sems
        self.tiles, self.sems = tiles, sems
        self.strided, self.near, self.share = [], [], []
        for i, stage in enumerate(STAGES):
            b = pl.ds(STARTS[i], len(stage))
            own = tiles.at[b, grid.zhi, grid.par, grid.core, grid.rghi, grid.rglo]
            self.strided.append([
                remote(own, own, a_s.at[i], a_r.at[i], grid.on_ring(4 * k)) for k in (2, 1, 3)
            ])
            four = tiles.at[b, :, grid.par, grid.core, :, grid.rglo]
            self.near.append([
                remote(four, four, b_s.at[i], b_r.at[i], grid.on_ring(d)) for d in (2, 1, -1)
            ])
            all_mine = tiles.at[b, :, :, grid.core]
            self.share.append(remote(all_mine, all_mine, c_s.at[i], c_r.at[i], grid.sibling()))

    def like(self, i, near):
        count = pl.ds(0, 3 * len(STAGES[i]) // 2)
        return self.tiles.at[count, 0, 0] if near else self.tiles.at[count, 0, 0, 0, 0]

    def begin(self, i):
        for copy in self.strided[i]:
            copy.start()

    def to_near(self, i):
        await_recv(self.like(i, False), self.sems[1].at[i])
        for copy in self.near[i]:
            copy.start()

    def to_sibling(self, i):
        await_recv(self.like(i, True), self.sems[3].at[i])
        self.share[i].start()

    def arrived(self, i):
        self.share[i].wait_recv()

    def sent(self):
        for i in range(len(STAGES)):
            await_recv(self.like(i, False), self.sems[0].at[i])
            await_recv(self.like(i, True), self.sems[2].at[i])
            self.share[i].wait_send()


def kernel(scale, cols, *refs):
    (
        key_ref, val_ref, cot_hbm, w_hbm, out_ref, grad_ref,
        w_ref, cot_ref, kall, kpair, left_ref, vc, vc_in, call, pm, vm, ptotal,
        p0, p1, p2, p3, p4, p5, s0, s1, s2, s3, s4, s5, tiles, rall, dall, acc_f, acc_o, acc_b, acc_g, comb, csend, osend, half,
        load_sem, swap_sem, wave0, wave1, wave2, c_send, c_recv,
        ps0, ps1, ps2, ps3, ps4, ps5, ss0, ss1, ss2, ss3, ss4, ss5, gs0, gs1, gs2, gs3, gs4, gs5,
        x_send, x_recv, f_send, f_recv, h_send, h_recv, o_send, o_recv, q_send, q_recv,
    ) = refs
    grid = Grid()
    zhi, core, a = grid.zhi, grid.core, grid.a
    mb, width = key_ref.shape[1], key_ref.shape[2]
    kmine, kother = kall.at[0], kall.at[1]
    rows = STEPS * mb

    loads = [pltpu.make_async_copy(w_hbm, w_ref, load_sem.at[0]), pltpu.make_async_copy(cot_hbm, cot_ref, load_sem.at[1])]
    for copy in loads:
        copy.start()
    targets = [grid.at_xy(*d) for d in XY] + [grid.sibling(), grid.pair()]
    targets += [grid.on_line(d) for d in range(1, DEPTH // 2)] + [grid.on_ring(d) for d in (4, 8, 12, 1, -1, -2)]
    targets += grid.sources()
    barrier = pltpu.get_barrier_semaphore()
    for device in targets:
        pl.semaphore_signal(barrier, inc=1, device_id=device, device_id_type=pl.DeviceIdType.MESH)

    kmine[:, a] = key_ref[...]
    key_rows = key_ref[...].reshape(rows, width)

    def padded(array):
        return jnp.concatenate([array, jnp.zeros(array.shape[:-1] + (LANES - cols,), array.dtype)], axis=-1)

    loads[0].wait()

    def project(zlo):
        columns = pl.ds(pl.multiple_of(zlo * (4 * cols), LANES), 4 * cols)
        block = jnp.dot(key_rows, w_ref[:, columns], preferred_element_type=F32)
        for c in range(2):
            for h in range(2):
                piece = padded(block[:, (2 * c + h) * cols:(2 * c + h + 1) * cols].astype(BF16))
                piece = piece.reshape(STEPS, mb // TILE, TILE, LANES)
                for t in range(STEPS):
                    p0[lax.div(zlo, 2), lax.rem(zlo, 2), c, pl.ds((2 * t + h) * (mb // TILE), mb // TILE)] = piece[t]

    repeat(0, DEPTH, project)
    loads[1].wait()
    window = cot_ref[:, :, pl.ds(pl.multiple_of(grid.zlo * (4 * cols), LANES), 4 * cols)]
    window = jnp.where(core == 0, window[:, :, :2 * cols], window[:, :, 2 * cols:])
    for h in range(2):
        vc[h, 0] = padded(val_ref[:, :, h * cols:(h + 1) * cols])
        vc[h, 1] = padded(window[:, :, h * cols:(h + 1) * cols])
    pl.semaphore_wait(barrier, len(targets))

    def key_swap(s):
        return remote(key_ref.at[s], kpair.at[s], swap_sem.at[0, s], swap_sem.at[1, s], grid.partner())

    waves = (wave0, wave1, wave2)
    early = Wave(grid, kmine, waves, 0, 0, 3)
    late = Wave(grid, kmine, waves, 1, 1, 2)
    across = [Wave(grid, kother, waves, 2, 0, 3), Wave(grid, kother, waves, 3, 1, 2)]
    key_swaps = [key_swap(s) for s in range(STEPS)]

    def vc_swap(number, which, t, count):
        part = pl.ds(t, count)
        return remote(
            vc.at[1 - zhi, which, part], vc_in.at[which, part], swap_sem.at[0, number], swap_sem.at[1, number],
            grid.partner(),
        )

    vc_swaps = [vc_swap(4, 0, 0, 1), vc_swap(5, 1, 3, 1), vc_swap(6, 0, 1, 3), vc_swap(7, 1, 0, 3)]
    first = 2 * mb // TILE
    p_swap = remote(ptotal.at[1 - zhi], pm.at[zhi], swap_sem.at[0, 8], swap_sem.at[1, 8], grid.partner())
    psum = LineSum(grid, (p0, p1, p2, p3, p4, p5), (ps0, ps1, ps2, ps3, ps4, ps5), [(0, STEPS * first)])
    scores = LineSum(
        grid, (s0, s1, s2, s3, s4, s5), (ss0, ss1, ss2, ss3, ss4, ss5), [(0, STARTS[1]), (STARTS[1], len(BLOCKS) - STARTS[1])]
    )
    ring = RingGather(grid, tiles, (gs0, gs1, gs2, gs3, gs4, gs5))

    def partial(s):
        right = kmine[s].reshape(AREA * mb, width)
        block = lax.dot_general(left_ref[...], right, (((1,), (1,)), ((), ())), preferred_element_type=F32).astype(BF16)
        for t in range(STEPS):
            b = BLOCKS.index((t, s))
            for group in range(4):
                for q in range(4):
                    row = (4 * t + group) * TILE
                    s0[group, q // 2, q % 2, b] = block[row:row + TILE, q * LANES:(q + 1) * LANES]

    def summed(i):
        b = pl.ds(*scores.ranges[i])
        tiles[b, zhi, grid.par, core, grid.rghi, grid.rglo] = scores.total(i).astype(BF16)

    def to_xy(mine, send, recv):
        def body(k):
            remote(mine, mine, send, recv, grid.at_xy(lax.div(k, SIDE), lax.rem(k, SIDE))).start()

        repeat(1, AREA, body)

    def exchange(store, index, number, value):
        store[index, :, a] = value
        to_xy(store.at[index, :, a], x_send.at[number], x_recv.at[number])
        return store.at[index, :, pl.ds(0, AREA - 1)], number

    def received(sent):
        await_recv(sent[0], x_recv.at[sent[1]])

    acc_f[...] = jnp.zeros_like(acc_f)
    acc_o[...] = jnp.zeros_like(acc_o)
    acc_b[...] = jnp.zeros_like(acc_b)

    def product(b, right):
        left = jnp.concatenate(
            [tiles[b, h, p, c].reshape(4 * TILE, LANES) for h in range(2) for p in range(2) for c in range(2)], axis=1
        )
        return jnp.dot(left, right.reshape(2 * AREA * mb, LANES), preferred_element_type=F32)

    def add_residual(t, s):
        term = product(BLOCKS.index((t, s)), rall[s])
        if t > s:
            acc_f[t] += (scale * momentum_sum(t - s)) * term
        acc_o[t] += (scale * momentum_sum(t + 1 - s)) * term

    def add_adjoint(s, t):
        acc_b[s] += (scale * momentum_sum(t - s)) * product(BLOCKS.index((s, t)), dall[t])

    def add_run(s, first, stop, store, later):
        base = BLOCKS.index((s, first)) - first

        def step(t, carry):
            factor, total = carry
            total = total + factor * product(base + t, store[t])
            return scale + MOMENTUM * factor, total

        factor = jnp.float32(scale * momentum_sum(first + later - s))
        acc_b[s] += lax.fori_loop(first, stop, step, (factor, jnp.zeros((2 * mb, LANES), F32)))[1]

    def projected(t):
        return pm[:, t].reshape(2 * mb, LANES).astype(F32)

    def residual(t):
        value = (projected(t) - acc_f[t] - vm[:, t].reshape(2 * mb, LANES).astype(F32)).astype(BF16)
        return exchange(rall, t, t, value.reshape(2, mb, LANES))

    def adjoint(s):
        value = (-acc_b[s]).astype(BF16).reshape(2, mb, LANES)
        copies = exchange(dall, s, STEPS + s, value) if s else None
        total = (value.astype(F32) + call[s, :, a].astype(F32)).astype(BF16)
        csend[s] = total
        x_hi, x_lo = lax.div(grid.x, 2), lax.rem(grid.x, 2)
        slot = comb.at[s, :, grid.y, x_hi, x_lo]

        def body(k):
            remote(csend.at[s], slot, f_send.at[s], f_recv.at[s], grid.owner(k)).start()

        repeat(0, DEPTH // 2, body)
        return copies

    def to_pair(s):
        held = comb.at[s, :, :, 1 - core, grid.par]
        await_recv(held, f_recv.at[s])
        passed[s] = remote(held, held, q_send.at[s], q_recv.at[s], grid.pair())
        passed[s].start()

    def to_core(s):
        passed[s].wait_recv()
        held = comb.at[s, :, :, 1 - core]
        shared[s] = remote(held, held, h_send.at[s], h_recv.at[s], grid.sibling())
        shared[s].start()

    def gradient(s):
        def body(h):
            which = h + zhi - 2 * h * zhi
            acc_g[...] += lax.dot_general(
                comb[s, which].reshape(AREA * mb, LANES), kall[h, s].reshape(AREA * mb, width),
                (((0,), (0,)), ((), ())), preferred_element_type=F32,
            )

        repeat(0, 2, body)

    def output(t):
        osend[:, t] = (projected(t) - acc_o[t]).astype(BF16).reshape(2, mb, LANES)
        half[zhi, t] = osend[zhi, t]
        copy = remote(osend.at[1 - zhi, t], half.at[zhi, t], o_send.at[t], o_recv.at[t], grid.partner())
        copy.start()
        return copy

    r_copies, d_copies, passed, shared, given = {}, {}, {}, {}, {}

    early.start()
    key_swaps[3].start()
    key_swaps[1].start()
    psum.begin(0)
    early.start_own()
    late.start()
    key_swaps[2].start()
    key_swaps[0].start()
    psum.to_pair(0)
    early.forward()
    late.start_own()
    late.forward()
    psum.to_line(0)
    for copy in vc_swaps:
        copy.start()
    early.arrived()
    late.arrived()
    for copy in key_swaps:
        copy.wait_recv()

    for t in range(STEPS):
        near, other = key_ref[t], kpair[t]
        left_ref[pl.ds(2 * t * mb, mb)] = jnp.where(zhi == 0, near, other)
        left_ref[pl.ds((2 * t + 1) * mb, mb)] = jnp.where(zhi == 0, other, near)
    for s in range(STEPS):
        partial(s)
    scores.begin(0)
    scores.begin(1)
    scores.to_pair(0)

    ptotal[...] = psum.total(0).reshape(STEPS, 2, mb, LANES).astype(BF16).transpose(1, 0, 2, 3)
    p_swap.start()
    pm[zhi] = ptotal[zhi]
    scores.to_line(0)
    for copy in vc_swaps:
        copy.wait_recv()

    def spread(number, t, count):
        part = pl.ds(t, count)
        call[part, zhi, a] = vc[zhi, 1, part]
        call[part, 1 - zhi, a] = vc_in[1, part]
        to_xy(call.at[part, :, a], c_send.at[number], c_recv.at[number])
        return call.at[part, :, pl.ds(0, AREA - 1)]

    vm[zhi] = vc[zhi, 0]
    vm[1 - zhi] = vc_in[0]
    all_c = [spread(0, 3, 1), spread(1, 0, 3)]
    scores.to_pair(1)
    summed(0)
    ring.begin(0)
    p_swap.wait_recv()
    r_copies[0] = residual(0)
    scores.to_line(1)
    kother[:, a] = kpair[...]
    ring.to_near(0)
    for wave in across:
        wave.start()
        wave.start_own()
    ring.to_sibling(0)
    for k in range(2):
        await_recv(all_c[k], c_recv.at[k])
    ring.arrived(0)

    add_run(3, 3, 4, call, 1)
    d_copies[3] = adjoint(3)
    received(r_copies[0])
    add_residual(1, 0)
    r_copies[1] = residual(1)
    summed(1)
    ring.begin(1)
    ring.begin(2)
    add_run(2, 2, 4, call, 1)
    add_residual(2, 0)

    received(d_copies[3])
    add_adjoint(2, 3)
    d_copies[2] = adjoint(2)
    received(r_copies[1])
    add_residual(2, 1)
    r_copies[2] = residual(2)
    ring.to_near(1)
    ring.to_near(2)
    for wave in across:
        wave.forward()
    to_pair(3)
    ring.to_sibling(1)
    ring.arrived(1)
    add_run(1, 1, 4, call, 1)
    add_adjoint(1, 3)
    add_residual(3, 0)
    add_residual(3, 1)

    received(d_copies[2])
    add_adjoint(1, 2)
    d_copies[1] = adjoint(1)
    received(r_copies[2])
    add_residual(3, 2)
    r_copies[3] = residual(3)
    ring.to_sibling(2)
    ring.arrived(2)
    to_core(3)
    to_pair(2)
    add_run(0, 0, 4, call, 1)
    add_run(0, 2, 4, dall, 0)

    received(d_copies[1])
    add_adjoint(0, 1)
    adjoint(0)
    for t in range(3):
        add_residual(t, t)
        given[t] = output(t)
    received(r_copies[3])
    add_residual(3, 3)
    given[3] = output(3)
    to_core(2)
    to_pair(1)
    for wave in across:
        wave.arrived()
    acc_g[...] = jnp.zeros_like(acc_g)
    shared[3].wait_recv()
    gradient(3)
    to_core(1)
    shared[2].wait_recv()
    gradient(2)
    shared[1].wait_recv()
    gradient(1)
    to_pair(0)
    to_core(0)
    for t in range(STEPS):
        given[t].wait_recv()
        out_ref[t] = jnp.concatenate([half[0, t][:, :cols], half[1, t][:, :cols]], axis=-1)
    shared[0].wait_recv()
    gradient(0)
    grad_ref[...] = acc_g[:cols].astype(BF16)

    early.sent()
    late.sent()
    for wave in across:
        wave.sent()
    psum.sent()
    scores.sent()
    ring.sent()
    for copy in key_swaps + vc_swaps + [p_swap] + list(given.values()) + list(passed.values()) + list(shared.values()):
        copy.wait_send()
    for k in range(2):
        await_recv(all_c[k], c_send.at[k])
    for like, number in list(r_copies.values()) + list(d_copies.values()):
        await_recv(like, x_send.at[number])
    for s in range(STEPS):
        await_recv(comb.at[s, :, :, 1 - core, grid.par], f_send.at[s])


def per_device(keys, values, cotangent, init_weight):
    steps, mb, width = keys.shape
    model_width = init_weight.shape[1]
    tok_count, tp_count = lax.axis_size("tok"), lax.axis_size("tp")
    cols = model_width // (2 * tp_count)
    hidden, batch_size = width * tp_count, mb * tok_count
    inner_rate = 0.5 * batch_size / (math.sqrt(hidden) + math.sqrt(batch_size)) ** 2
    scale = inner_rate / batch_size
    dma = pltpu.SemaphoreType.DMA
    rows = steps * mb
    blocks = 2 * rows // TILE

    def sums():
        return [
            pltpu.VMEM((4, 2, 2, blocks, TILE, LANES), BF16), pltpu.VMEM((4, 2, blocks, TILE, LANES), BF16),
        ] + [pltpu.VMEM((4, blocks, TILE, LANES), BF16)] * 4

    def sum_sems(count):
        return [dma((count,))] * 6

    own = (steps, 2, AREA, mb, LANES)
    half = (2, steps, mb, LANES)
    scratch = [
        pltpu.VMEM(init_weight.shape, BF16), pltpu.VMEM(cotangent.shape, BF16),
        pltpu.VMEM((2, steps, AREA, mb, width), BF16),
        pltpu.VMEM(keys.shape, BF16), pltpu.VMEM((2 * rows, width), BF16),
        pltpu.VMEM((2, 2, steps, mb, LANES), BF16), pltpu.VMEM((2, steps, mb, LANES), BF16),
        pltpu.VMEM(own, BF16), pltpu.VMEM(half, BF16), pltpu.VMEM(half, BF16), pltpu.VMEM(half, BF16),
        *sums(), *sums(),
        pltpu.VMEM((16, 2, 2, 2, 2, 2, TILE, LANES), BF16),
        pltpu.VMEM(own, BF16), pltpu.VMEM(own, BF16),
        pltpu.VMEM((steps, 2 * mb, LANES), F32), pltpu.VMEM((steps, 2 * mb, LANES), F32),
        pltpu.VMEM((steps, 2 * mb, LANES), F32), pltpu.VMEM((LANES, width), F32),
        pltpu.VMEM((steps, 2, SIDE, 2, SIDE // 2, mb, LANES), BF16), pltpu.VMEM((steps, 2, mb, LANES), BF16),
        pltpu.VMEM(half, BF16), pltpu.VMEM(half, BF16),
        dma((2,)), dma((2, steps + 6)),
        dma((4,)), dma((4, 2)), dma((4,)), dma((2,)), dma((2,)),
        *sum_sems(1), *sum_sems(2),
        *[dma((len(STAGES),))] * 6,
        dma((2 * steps,)), dma((2 * steps,)),
        *[dma((steps,))] * 8,
    ]
    vmem, hbm = pl.BlockSpec(memory_space=pltpu.VMEM), pl.BlockSpec(memory_space=pl.ANY)
    out, grad = pl.pallas_call(
        functools.partial(kernel, scale, cols),
        name="step",
        out_shape=[
            jax.ShapeDtypeStruct((steps, mb, 2 * cols), BF16), jax.ShapeDtypeStruct((cols, width), BF16),
        ],
        in_specs=[vmem, vmem, hbm, hbm],
        out_specs=[vmem, vmem],
        scratch_shapes=scratch,
        compiler_params=pltpu.CompilerParams(collective_id=0, has_side_effects=True, vmem_limit_bytes=VMEM_LIMIT),
    )(keys, values, cotangent, init_weight)
    return out, grad.T


def solution(mesh):
    return jax.shard_map(
        per_device,
        mesh=mesh,
        in_specs=(P(None, "tok", "tp"), P(None, "tok", "tp"), P(None, "tok", None), P("tp", None)),
        out_specs=(P(None, "tok", "tp"), P("tp", "tok")),
        check_vma=False,
    )
```

```python
import functools
import math

import jax
import jax.numpy as jnp
from jax import lax
from jax.experimental import pallas as pl
from jax.experimental.pallas import tpu as pltpu
from jax.sharding import PartitionSpec as P

MOMENTUM = 0.9
LANES = 128
TILE = 16
F32 = jnp.float32
BF16 = jnp.bfloat16
VMEM_LIMIT = 56 * 1024 * 1024
STEPS = 4
SIDE = 4
DEPTH = 8
AREA = SIDE * SIDE
STAGES = (
    ((1, 0), (3, 3), (2, 0), (2, 1), (2, 2), (2, 3)),
    ((3, 0), (3, 1), (3, 2), (1, 1), (1, 2), (1, 3)),
    ((0, 0), (0, 1), (0, 2), (0, 3)),
)
BLOCKS = [block for stage in STAGES for block in stage]
STARTS = [sum(len(stage) for stage in STAGES[:i]) for i in range(len(STAGES))]


def momentum_sum(count):
    return (1.0 - MOMENTUM**count) / (1.0 - MOMENTUM)


class Grid:
    def __init__(self):
        tok, tp = lax.axis_index("tok"), lax.axis_index("tp")
        self.tok, self.tp = tok, tp
        self.y = lax.div(tok, 2 * SIDE)
        self.zhi = lax.rem(lax.div(tok, SIDE), 2)
        self.x = lax.rem(tok, SIDE)
        self.zlo = lax.div(tp, 2)
        self.core = lax.rem(tp, 2)
        self.a = self.y * SIDE + self.x
        self.z = self.zhi * DEPTH + self.zlo
        self.group = lax.div(self.zlo, 2)
        self.par = lax.rem(self.zlo, 2)
        self.rghi = lax.div(self.zlo, 4)
        self.rglo = lax.rem(self.group, 2)

    def tok_of(self, y, zhi, x):
        return y * (2 * SIDE) + zhi * SIDE + x

    def at_xy(self, dy, dx):
        y = lax.rem(self.y + dy + SIDE, SIDE)
        x = lax.rem(self.x + dx + SIDE, SIDE)
        return (self.tok_of(y, self.zhi, x), self.tp)

    def a_at(self, dy, dx):
        y = lax.rem(self.y + dy + SIDE, SIDE)
        x = lax.rem(self.x + dx + SIDE, SIDE)
        return y * SIDE + x

    def partner(self):
        return (self.tok_of(self.y, 1 - self.zhi, self.x), self.tp)

    def sibling(self):
        return (self.tok, self.zlo * 2 + 1 - self.core)

    def pair(self):
        return (self.tok, (self.zlo + 1 - 2 * self.par) * 2 + self.core)

    def group_at(self, d):
        return lax.rem(self.group + d + DEPTH // 2, DEPTH // 2)

    def on_line(self, d):
        return (self.tok, (self.group_at(d) * 2 + self.par) * 2 + self.core)

    def on_ring(self, d):
        z = lax.rem(self.z + d + 2 * DEPTH, 2 * DEPTH)
        zhi, zlo = lax.div(z, DEPTH), lax.rem(z, DEPTH)
        return (self.tok_of(self.y, zhi, self.x), zlo * 2 + self.core)

    def owner(self, k):
        zlo = lax.rem(self.group + k, DEPTH // 2) * 2 + lax.rem(self.x, 2)
        return (2 * self.tp + self.zhi, zlo * 2 + 1 - lax.div(self.x, 2))


XY = [(dy, dx) for dy in range(SIDE) for dx in range(SIDE) if (dy, dx) != (0, 0)]


def remote(src, dst, send, recv, device):
    return pltpu.make_async_remote_copy(
        src_ref=src, dst_ref=dst, send_sem=send, recv_sem=recv, device_id=device, device_id_type=pl.DeviceIdType.MESH
    )


def repeat(first, stop, body):
    def step(i, carry):
        body(i)
        return carry

    lax.fori_loop(first, stop, step, 0)


def await_recv(like, sem):
    pltpu.make_async_copy(like, like, sem).wait()


class Wave:
    def __init__(self, grid, blocks, sems, number, first, second):
        self.grid, self.blocks, self.steps = grid, blocks, (first, second)
        self.send, self.recv1, self.recv2 = [sem.at[number] for sem in sems]

    def along(self, h, d):
        return (d, 0) if h == 0 else (0, d)

    def start(self):
        def body(d):
            for h in range(2):
                mine = self.blocks.at[self.steps[h], self.grid.a]
                remote(mine, mine, self.send, self.recv1.at[h], self.grid.at_xy(*self.along(h, d))).start()

        repeat(1, SIDE, body)

    def pass_on(self, h, d, e):
        held = self.blocks.at[self.steps[h], self.grid.a_at(*self.along(h, -d))]
        remote(held, held, self.send, self.recv2, self.grid.at_xy(*self.along(1 - h, e))).start()

    def start_own(self):
        def body(e):
            for h in range(2):
                self.pass_on(h, 0, e)

        repeat(1, SIDE, body)

    def forward(self):
        for h in range(2):
            await_recv(self.blocks.at[0, pl.ds(0, SIDE - 1)], self.recv1.at[h])
            count = SIDE - 1
            repeat(0, count * count, lambda k, h=h: self.pass_on(h, lax.div(k, count) + 1, lax.rem(k, count) + 1))

    def arrived(self):
        await_recv(self.blocks.at[pl.ds(0, 2), pl.ds(0, SIDE * (SIDE - 1))], self.recv2)

    def sent(self):
        await_recv(self.blocks.at[pl.ds(0, 2), pl.ds(0, (SIDE + 1) * (SIDE - 1))], self.send)


class LineSum:
    def __init__(self, grid, bufs, sems, ranges):
        self.grid, self.ranges = grid, ranges
        self.part, self.sib, self.stage1, self.pair, self.stage2, self.recv = bufs
        sib_s, sib_r, pair_s, pair_r, line_s, line_r = sems
        self.sib_copy, self.pair_copy = [], []
        self.line_s, self.line_r = line_s, line_r
        for i, (start, size) in enumerate(ranges):
            b = pl.ds(start, size)
            self.sib_copy.append(remote(
                self.part.at[:, :, 1 - grid.core, b], self.sib.at[:, :, b], sib_s.at[i], sib_r.at[i], grid.sibling()
            ))
            self.pair_copy.append(remote(
                self.stage1.at[:, b], self.pair.at[:, b], pair_s.at[i], pair_r.at[i], grid.pair()
            ))

    def begin(self, i):
        self.sib_copy[i].start()

    def to_pair(self, i):
        grid, b = self.grid, pl.ds(*self.ranges[i])
        self.sib_copy[i].wait_recv()
        other = 1 - grid.par

        def body(group):
            own = self.part[group, other, grid.core, b].astype(F32) + self.sib[group, other, b].astype(F32)
            self.stage1[group, b] = own.astype(BF16)

        repeat(0, DEPTH // 2, body)
        self.pair_copy[i].start()

    def chip_sum(self, group, b):
        grid = self.grid
        own = self.part[group, grid.par, grid.core, b].astype(F32) + self.sib[group, grid.par, b].astype(F32)
        return own + self.pair[group, b].astype(F32)

    def to_line(self, i):
        grid, b = self.grid, pl.ds(*self.ranges[i])
        self.pair_copy[i].wait_recv()

        def body(d):
            self.stage2[d, b] = self.chip_sum(grid.group_at(d), b).astype(BF16)
            remote(self.stage2.at[d, b], self.recv.at[d, b], self.line_s.at[i], self.line_r.at[i], grid.on_line(d)).start()

        repeat(1, DEPTH // 2, body)

    def total(self, i):
        b = pl.ds(*self.ranges[i])
        total = self.chip_sum(self.grid.group, b)
        await_recv(self.recv.at[pl.ds(1, DEPTH // 2 - 1), b], self.line_r.at[i])
        for d in range(1, DEPTH // 2):
            total = total + self.recv[d, b].astype(F32)
        return total

    def sent(self):
        for i in range(len(self.ranges)):
            self.sib_copy[i].wait_send()
            self.pair_copy[i].wait_send()
            await_recv(self.stage2.at[pl.ds(1, DEPTH // 2 - 1), pl.ds(*self.ranges[i])], self.line_s.at[i])


class RingGather:
    def __init__(self, grid, tiles, sems):
        a_s, a_r, b_s, b_r, c_s, c_r = sems
        self.tiles, self.sems = tiles, sems
        self.strided, self.near, self.share = [], [], []
        for i, stage in enumerate(STAGES):
            b = pl.ds(STARTS[i], len(stage))
            own = tiles.at[b, grid.zhi, grid.par, grid.core, grid.rghi, grid.rglo]
            self.strided.append([
                remote(own, own, a_s.at[i], a_r.at[i], grid.on_ring(4 * k)) for k in (2, 1, 3)
            ])
            four = tiles.at[b, :, grid.par, grid.core, :, grid.rglo]
            self.near.append([
                remote(four, four, b_s.at[i], b_r.at[i], grid.on_ring(d)) for d in (2, 1, -1)
            ])
            all_mine = tiles.at[b, :, :, grid.core]
            self.share.append(remote(all_mine, all_mine, c_s.at[i], c_r.at[i], grid.sibling()))

    def like(self, i, near):
        count = pl.ds(0, 3 * len(STAGES[i]) // 2)
        return self.tiles.at[count, 0, 0] if near else self.tiles.at[count, 0, 0, 0, 0]

    def begin(self, i):
        for copy in self.strided[i]:
            copy.start()

    def to_near(self, i):
        await_recv(self.like(i, False), self.sems[1].at[i])
        for copy in self.near[i]:
            copy.start()

    def to_sibling(self, i):
        await_recv(self.like(i, True), self.sems[3].at[i])
        self.share[i].start()

    def arrived(self, i):
        self.share[i].wait_recv()

    def sent(self):
        for i in range(len(STAGES)):
            await_recv(self.like(i, False), self.sems[0].at[i])
            await_recv(self.like(i, True), self.sems[2].at[i])
            self.share[i].wait_send()


def kernel(scale, cols, *refs):
    (
        key_ref, val_ref, cot_hbm, w_hbm, out_ref, grad_ref,
        w_ref, cot_ref, kall, kpair, left_ref, vc, vc_in, call, pm, vm, ptotal,
        p0, p1, p2, p3, p4, p5, s0, s1, s2, s3, s4, s5, tiles, rall, dall, acc_f, acc_o, acc_b, acc_g, comb, csend, osend, half,
        load_sem, swap_sem, wave0, wave1, wave2, c_send, c_recv,
        ps0, ps1, ps2, ps3, ps4, ps5, ss0, ss1, ss2, ss3, ss4, ss5, gs0, gs1, gs2, gs3, gs4, gs5,
        x_send, x_recv, f_send, f_recv, h_send, h_recv, o_send, o_recv, q_send, q_recv,
    ) = refs
    grid = Grid()
    zhi, core, a = grid.zhi, grid.core, grid.a
    mb, width = key_ref.shape[1], key_ref.shape[2]
    kmine, kother = kall.at[0], kall.at[1]
    rows = STEPS * mb

    loads = [pltpu.make_async_copy(w_hbm, w_ref, load_sem.at[0]), pltpu.make_async_copy(cot_hbm, cot_ref, load_sem.at[1])]
    for copy in loads:
        copy.start()
    targets = [grid.at_xy(*d) for d in XY] + [grid.sibling(), grid.pair()]
    targets += [grid.on_line(d) for d in range(1, DEPTH // 2)] + [grid.on_ring(d) for d in (4, 8, 12, 1, -1, -2)]
    barrier = pltpu.get_barrier_semaphore()
    for device in targets:
        pl.semaphore_signal(barrier, inc=1, device_id=device, device_id_type=pl.DeviceIdType.MESH)

    kmine[:, a] = key_ref[...]
    key_rows = key_ref[...].reshape(rows, width)

    def padded(array):
        return jnp.concatenate([array, jnp.zeros(array.shape[:-1] + (LANES - cols,), array.dtype)], axis=-1)

    loads[0].wait()

    def project(zlo):
        columns = pl.ds(pl.multiple_of(zlo * (4 * cols), LANES), 4 * cols)
        block = jnp.dot(key_rows, w_ref[:, columns], preferred_element_type=F32)
        for c in range(2):
            for h in range(2):
                piece = padded(block[:, (2 * c + h) * cols:(2 * c + h + 1) * cols].astype(BF16))
                piece = piece.reshape(STEPS, mb // TILE, TILE, LANES)
                for t in range(STEPS):
                    p0[lax.div(zlo, 2), lax.rem(zlo, 2), c, pl.ds((2 * t + h) * (mb // TILE), mb // TILE)] = piece[t]

    repeat(0, DEPTH, project)
    loads[1].wait()
    window = cot_ref[:, :, pl.ds(pl.multiple_of(grid.zlo * (4 * cols), LANES), 4 * cols)]
    window = jnp.where(core == 0, window[:, :, :2 * cols], window[:, :, 2 * cols:])
    for h in range(2):
        vc[h, 0] = padded(val_ref[:, :, h * cols:(h + 1) * cols])
        vc[h, 1] = padded(window[:, :, h * cols:(h + 1) * cols])
    pl.semaphore_wait(barrier, len(targets))

    def key_swap(s):
        return remote(key_ref.at[s], kpair.at[s], swap_sem.at[0, s], swap_sem.at[1, s], grid.partner())

    waves = (wave0, wave1, wave2)
    early = Wave(grid, kmine, waves, 0, 0, 3)
    late = Wave(grid, kmine, waves, 1, 1, 2)
    across = [Wave(grid, kother, waves, 2, 0, 3), Wave(grid, kother, waves, 3, 1, 2)]
    key_swaps = [key_swap(s) for s in range(STEPS)]

    def vc_swap(number, which, t, count):
        part = pl.ds(t, count)
        return remote(
            vc.at[1 - zhi, which, part], vc_in.at[which, part], swap_sem.at[0, number], swap_sem.at[1, number],
            grid.partner(),
        )

    vc_swaps = [vc_swap(4, 0, 0, 1), vc_swap(5, 1, 3, 1), vc_swap(6, 0, 1, 3), vc_swap(7, 1, 0, 3)]
    first = 2 * mb // TILE
    p_swap = remote(ptotal.at[1 - zhi], pm.at[zhi], swap_sem.at[0, 8], swap_sem.at[1, 8], grid.partner())
    psum = LineSum(grid, (p0, p1, p2, p3, p4, p5), (ps0, ps1, ps2, ps3, ps4, ps5), [(0, STEPS * first)])
    scores = LineSum(
        grid, (s0, s1, s2, s3, s4, s5), (ss0, ss1, ss2, ss3, ss4, ss5), [(0, STARTS[1]), (STARTS[1], len(BLOCKS) - STARTS[1])]
    )
    ring = RingGather(grid, tiles, (gs0, gs1, gs2, gs3, gs4, gs5))

    def partial(s):
        right = kmine[s].reshape(AREA * mb, width)
        block = lax.dot_general(left_ref[...], right, (((1,), (1,)), ((), ())), preferred_element_type=F32).astype(BF16)
        for t in range(STEPS):
            b = BLOCKS.index((t, s))
            for group in range(4):
                for q in range(4):
                    row = (4 * t + group) * TILE
                    s0[group, q // 2, q % 2, b] = block[row:row + TILE, q * LANES:(q + 1) * LANES]

    def summed(i):
        b = pl.ds(*scores.ranges[i])
        tiles[b, zhi, grid.par, core, grid.rghi, grid.rglo] = scores.total(i).astype(BF16)

    def to_xy(mine, send, recv):
        def body(k):
            remote(mine, mine, send, recv, grid.at_xy(lax.div(k, SIDE), lax.rem(k, SIDE))).start()

        repeat(1, AREA, body)

    def exchange(store, index, number, value):
        store[index, :, a] = value
        to_xy(store.at[index, :, a], x_send.at[number], x_recv.at[number])
        return store.at[index, :, pl.ds(0, AREA - 1)], number

    def received(sent):
        await_recv(sent[0], x_recv.at[sent[1]])

    acc_f[...] = jnp.zeros_like(acc_f)
    acc_o[...] = jnp.zeros_like(acc_o)
    acc_b[...] = jnp.zeros_like(acc_b)

    def product(b, right):
        left = jnp.concatenate(
            [tiles[b, h, p, c].reshape(4 * TILE, LANES) for h in range(2) for p in range(2) for c in range(2)], axis=1
        )
        return jnp.dot(left, right.reshape(2 * AREA * mb, LANES), preferred_element_type=F32)

    def add_residual(t, s):
        term = product(BLOCKS.index((t, s)), rall[s])
        if t > s:
            acc_f[t] += (scale * momentum_sum(t - s)) * term
        acc_o[t] += (scale * momentum_sum(t + 1 - s)) * term

    def add_adjoint(s, t):
        acc_b[s] += (scale * momentum_sum(t - s)) * product(BLOCKS.index((s, t)), dall[t])

    def add_run(s, first, stop, store, later):
        base = BLOCKS.index((s, first)) - first

        def step(t, carry):
            factor, total = carry
            total = total + factor * product(base + t, store[t])
            return scale + MOMENTUM * factor, total

        factor = jnp.float32(scale * momentum_sum(first + later - s))
        acc_b[s] += lax.fori_loop(first, stop, step, (factor, jnp.zeros((2 * mb, LANES), F32)))[1]

    def projected(t):
        return pm[:, t].reshape(2 * mb, LANES).astype(F32)

    def residual(t):
        value = (projected(t) - acc_f[t] - vm[:, t].reshape(2 * mb, LANES).astype(F32)).astype(BF16)
        return exchange(rall, t, t, value.reshape(2, mb, LANES))

    def adjoint(s):
        value = (-acc_b[s]).astype(BF16).reshape(2, mb, LANES)
        copies = exchange(dall, s, STEPS + s, value) if s else None
        total = (value.astype(F32) + call[s, :, a].astype(F32)).astype(BF16)
        csend[s] = total
        x_hi, x_lo = lax.div(grid.x, 2), lax.rem(grid.x, 2)
        slot = comb.at[s, :, grid.y, x_hi, x_lo]

        def body(k):
            remote(csend.at[s], slot, f_send.at[s], f_recv.at[s], grid.owner(k)).start()

        repeat(0, DEPTH // 2, body)
        return copies

    def to_pair(s):
        held = comb.at[s, :, :, 1 - core, grid.par]
        await_recv(held, f_recv.at[s])
        passed[s] = remote(held, held, q_send.at[s], q_recv.at[s], grid.pair())
        passed[s].start()

    def to_core(s):
        passed[s].wait_recv()
        held = comb.at[s, :, :, 1 - core]
        shared[s] = remote(held, held, h_send.at[s], h_recv.at[s], grid.sibling())
        shared[s].start()

    def gradient(s):
        def body(h):
            which = h + zhi - 2 * h * zhi
            acc_g[...] += lax.dot_general(
                comb[s, which].reshape(AREA * mb, LANES), kall[h, s].reshape(AREA * mb, width),
                (((0,), (0,)), ((), ())), preferred_element_type=F32,
            )

        repeat(0, 2, body)

    def output(t):
        osend[:, t] = (projected(t) - acc_o[t]).astype(BF16).reshape(2, mb, LANES)
        half[zhi, t] = osend[zhi, t]
        copy = remote(osend.at[1 - zhi, t], half.at[zhi, t], o_send.at[t], o_recv.at[t], grid.partner())
        copy.start()
        return copy

    r_copies, d_copies, passed, shared, given = {}, {}, {}, {}, {}

    early.start()
    key_swaps[3].start()
    key_swaps[1].start()
    psum.begin(0)
    early.start_own()
    late.start()
    key_swaps[2].start()
    key_swaps[0].start()
    psum.to_pair(0)
    early.forward()
    late.start_own()
    late.forward()
    psum.to_line(0)
    for copy in vc_swaps:
        copy.start()
    early.arrived()
    late.arrived()
    for copy in key_swaps:
        copy.wait_recv()

    for t in range(STEPS):
        near, other = key_ref[t], kpair[t]
        left_ref[pl.ds(2 * t * mb, mb)] = jnp.where(zhi == 0, near, other)
        left_ref[pl.ds((2 * t + 1) * mb, mb)] = jnp.where(zhi == 0, other, near)
    for s in range(STEPS):
        partial(s)
    scores.begin(0)
    scores.begin(1)
    scores.to_pair(0)

    ptotal[...] = psum.total(0).reshape(STEPS, 2, mb, LANES).astype(BF16).transpose(1, 0, 2, 3)
    p_swap.start()
    pm[zhi] = ptotal[zhi]
    scores.to_line(0)
    for copy in vc_swaps:
        copy.wait_recv()

    def spread(number, t, count):
        part = pl.ds(t, count)
        call[part, zhi, a] = vc[zhi, 1, part]
        call[part, 1 - zhi, a] = vc_in[1, part]
        to_xy(call.at[part, :, a], c_send.at[number], c_recv.at[number])
        return call.at[part, :, pl.ds(0, AREA - 1)]

    vm[zhi] = vc[zhi, 0]
    vm[1 - zhi] = vc_in[0]
    all_c = [spread(0, 3, 1), spread(1, 0, 3)]
    scores.to_pair(1)
    summed(0)
    ring.begin(0)
    p_swap.wait_recv()
    r_copies[0] = residual(0)
    scores.to_line(1)
    kother[:, a] = kpair[...]
    ring.to_near(0)
    for wave in across:
        wave.start()
        wave.start_own()
    ring.to_sibling(0)
    for k in range(2):
        await_recv(all_c[k], c_recv.at[k])
    ring.arrived(0)

    add_run(3, 3, 4, call, 1)
    d_copies[3] = adjoint(3)
    received(r_copies[0])
    add_residual(1, 0)
    r_copies[1] = residual(1)
    summed(1)
    ring.begin(1)
    ring.begin(2)
    add_run(2, 2, 4, call, 1)
    add_residual(2, 0)

    received(d_copies[3])
    add_adjoint(2, 3)
    d_copies[2] = adjoint(2)
    received(r_copies[1])
    add_residual(2, 1)
    r_copies[2] = residual(2)
    ring.to_near(1)
    ring.to_near(2)
    for wave in across:
        wave.forward()
    to_pair(3)
    ring.to_sibling(1)
    ring.arrived(1)
    add_run(1, 1, 4, call, 1)
    add_adjoint(1, 3)
    add_residual(3, 0)
    add_residual(3, 1)

    received(d_copies[2])
    add_adjoint(1, 2)
    d_copies[1] = adjoint(1)
    received(r_copies[2])
    add_residual(3, 2)
    r_copies[3] = residual(3)
    ring.to_sibling(2)
    ring.arrived(2)
    to_core(3)
    to_pair(2)
    add_run(0, 0, 4, call, 1)
    add_run(0, 2, 4, dall, 0)

    received(d_copies[1])
    add_adjoint(0, 1)
    adjoint(0)
    for t in range(3):
        add_residual(t, t)
        given[t] = output(t)
    received(r_copies[3])
    add_residual(3, 3)
    given[3] = output(3)
    to_core(2)
    to_pair(1)
    for wave in across:
        wave.arrived()
    acc_g[...] = jnp.zeros_like(acc_g)
    shared[3].wait_recv()
    gradient(3)
    to_core(1)
    shared[2].wait_recv()
    gradient(2)
    shared[1].wait_recv()
    gradient(1)
    to_pair(0)
    to_core(0)
    for t in range(STEPS):
        given[t].wait_recv()
        out_ref[t] = jnp.concatenate([half[0, t][:, :cols], half[1, t][:, :cols]], axis=-1)
    shared[0].wait_recv()
    gradient(0)
    grad_ref[...] = acc_g[:cols].astype(BF16)

    early.sent()
    late.sent()
    for wave in across:
        wave.sent()
    psum.sent()
    scores.sent()
    ring.sent()
    for copy in key_swaps + vc_swaps + [p_swap] + list(given.values()) + list(passed.values()) + list(shared.values()):
        copy.wait_send()
    for k in range(2):
        await_recv(all_c[k], c_send.at[k])
    for like, number in list(r_copies.values()) + list(d_copies.values()):
        await_recv(like, x_send.at[number])
    for s in range(STEPS):
        await_recv(comb.at[s, :, :, 1 - core, grid.par], f_send.at[s])


def per_device(keys, values, cotangent, init_weight):
    steps, mb, width = keys.shape
    model_width = init_weight.shape[1]
    tok_count, tp_count = lax.axis_size("tok"), lax.axis_size("tp")
    cols = model_width // (2 * tp_count)
    hidden, batch_size = width * tp_count, mb * tok_count
    inner_rate = 0.5 * batch_size / (math.sqrt(hidden) + math.sqrt(batch_size)) ** 2
    scale = inner_rate / batch_size
    dma = pltpu.SemaphoreType.DMA
    rows = steps * mb
    blocks = 2 * rows // TILE

    def sums():
        return [
            pltpu.VMEM((4, 2, 2, blocks, TILE, LANES), BF16), pltpu.VMEM((4, 2, blocks, TILE, LANES), BF16),
        ] + [pltpu.VMEM((4, blocks, TILE, LANES), BF16)] * 4

    def sum_sems(count):
        return [dma((count,))] * 6

    own = (steps, 2, AREA, mb, LANES)
    half = (2, steps, mb, LANES)
    scratch = [
        pltpu.VMEM(init_weight.shape, BF16), pltpu.VMEM(cotangent.shape, BF16),
        pltpu.VMEM((2, steps, AREA, mb, width), BF16),
        pltpu.VMEM(keys.shape, BF16), pltpu.VMEM((2 * rows, width), BF16),
        pltpu.VMEM((2, 2, steps, mb, LANES), BF16), pltpu.VMEM((2, steps, mb, LANES), BF16),
        pltpu.VMEM(own, BF16), pltpu.VMEM(half, BF16), pltpu.VMEM(half, BF16), pltpu.VMEM(half, BF16),
        *sums(), *sums(),
        pltpu.VMEM((16, 2, 2, 2, 2, 2, TILE, LANES), BF16),
        pltpu.VMEM(own, BF16), pltpu.VMEM(own, BF16),
        pltpu.VMEM((steps, 2 * mb, LANES), F32), pltpu.VMEM((steps, 2 * mb, LANES), F32),
        pltpu.VMEM((steps, 2 * mb, LANES), F32), pltpu.VMEM((LANES, width), F32),
        pltpu.VMEM((steps, 2, SIDE, 2, SIDE // 2, mb, LANES), BF16), pltpu.VMEM((steps, 2, mb, LANES), BF16),
        pltpu.VMEM(half, BF16), pltpu.VMEM(half, BF16),
        dma((2,)), dma((2, steps + 6)),
        dma((4,)), dma((4, 2)), dma((4,)), dma((2,)), dma((2,)),
        *sum_sems(1), *sum_sems(2),
        *[dma((len(STAGES),))] * 6,
        dma((2 * steps,)), dma((2 * steps,)),
        *[dma((steps,))] * 8,
    ]
    vmem, hbm = pl.BlockSpec(memory_space=pltpu.VMEM), pl.BlockSpec(memory_space=pl.ANY)
    out, grad = pl.pallas_call(
        functools.partial(kernel, scale, cols),
        name="step",
        out_shape=[
            jax.ShapeDtypeStruct((steps, mb, 2 * cols), BF16), jax.ShapeDtypeStruct((cols, width), BF16),
        ],
        in_specs=[vmem, vmem, hbm, hbm],
        out_specs=[vmem, vmem],
        scratch_shapes=scratch,
        compiler_params=pltpu.CompilerParams(collective_id=0, has_side_effects=True, vmem_limit_bytes=VMEM_LIMIT),
    )(keys, values, cotangent, init_weight)
    return out, grad.T


def solution(mesh):
    return jax.shard_map(
        per_device,
        mesh=mesh,
        in_specs=(P(None, "tok", "tp"), P(None, "tok", "tp"), P(None, "tok", None), P("tp", None)),
        out_specs=(P(None, "tok", "tp"), P("tp", "tok")),
        check_vma=False,
    )
```
